256 devices in a mesh: segment: 8 (over z_hi, x), seq: 32 (over z_lo, y, core).
Axes of the slice: x: 4, y: 4, z: 8 (z_hi: 2, z_lo: 4; z = z_hi * 4 + z_lo), core: 2. Of those that a mesh axis runs over, the one named last changes fastest.
Arguments:
- queries: bfloat16 [24576, 3072], P('seq', 'segment'), may hold values from -9 to 9
- key_rows: bfloat16 [24576, 3072], P('seq', 'segment'), may hold values from -6 to 6
- value_rows: bfloat16 [24576, 3072], P('seq', 'segment'), may hold values from -6 to 6
- neighbours: int32 [64, 4], P('seq'), may hold values from 0 to 63, as said below
- tile_counts: int32 [64], P('seq'), may hold values from 2 to 4
- panels: bfloat16 [24576, 12288], P('seq', 'segment'), may hold values from -3 to 3
- alignment: bfloat16 [3072, 3072], P('segment'), may hold values from -0.5 to 0.5
- tap_pick: int32 [64], P('seq'), may hold values from 0 to 3
Outputs:
- grad_align: float32 [3072, 3072], P('segment', 'seq')
- grad_attn: bfloat16 [24576, 3072], P('seq', 'segment')
The draws below stay inside these ranges and needn't reach their ends.
Inputs may be any that keep to these rules, and one draw needn't show every extreme that they name: `neighbours`: row t starts with t itself; its other entries are distinct tiles of the same index of seq as t or of the index before or after it, 2 tiles to an index in order.
All inputs are finite; a program needn't handle non-finite values.
Results may differ from the reference program's by a relative error of at most 0.017.
Values may be sent and summed in bfloat16 or wider, within the bound.
No kernel may reach another device: no remote copies, remote signals or barrier semaphores. Data moves between devices by JAX's collectives and lax.ppermute only.
A program may use at most 128 MiB of HBM per device.

```python
import jax
import jax.numpy as jnp
from jax import lax

HEADS = 24
HDIM = 128
D = 3072
TILE = 384
TPD = 2
NB = 4
SECTIONS = 4
GROUPS = 8
PANEL_COLS = 1536
TILES = 64
TOKENS = 24576


def query_key_common(key):
    base = jax.random.fold_in(key, 11)
    key_query, key_keys = jax.random.split(base, 2)
    row_total = TOKENS
    row_width = HEADS * HDIM
    queries = jax.random.truncated_normal(key_query, -6.0, 6.0, (row_total, row_width), jnp.float32)
    key_vals = jax.random.truncated_normal(key_keys, -6.0, 6.0, (row_total, row_width), jnp.float32)
    return (queries, key_vals)


def draw_queries(key, part):
    return query_key_common(key)[0].astype(jnp.bfloat16)


def draw_key_rows(key, part):
    return query_key_common(key)[1].astype(jnp.bfloat16)


def tile_common(key):
    base = jax.random.fold_in(key, 23)
    key_order, key_count = jax.random.split(base, 2)
    tile_ids = jnp.arange(TILES, dtype=jnp.int32)
    owner = tile_ids // TPD
    cand_pos = jnp.arange(3 * TPD, dtype=jnp.int32)
    candidates = (owner[:, None] - 1) * TPD + cand_pos[None, :]
    usable = (candidates >= 0) & (candidates < TILES) & (candidates != tile_ids[:, None])
    noise = jax.random.randint(key_order, (TILES, 3 * TPD), 0, 65536, dtype=jnp.int32)
    ranking = noise * (4 * TPD) + cand_pos[None, :] + jnp.where(usable, 0, 1 << 28)
    order = jnp.argsort(ranking, axis=1, stable=True)
    picked = jnp.take_along_axis(candidates, order, axis=1)[:, :NB - 1]
    lists = jnp.concatenate([tile_ids[:, None], picked], axis=1).astype(jnp.int32)
    used = jax.random.randint(key_count, (TILES,), 2, NB + 1, dtype=jnp.int32)
    used = used.at[0].set(2)
    used = used.at[TILES - 1].set(NB)
    return (lists, used)


def draw_neighbours(key, part):
    return tile_common(key)[0]


def draw_tile_counts(key, part):
    return tile_common(key)[1]


def with_ends(array, stream_key, least, high):
    place = [jax.random.randint(jax.random.fold_in(stream_key, axis), (), 0, length) for axis, length in enumerate(array.shape)]
    widest = array.shape.index(max(array.shape))
    neighbour = place[:widest] + [(place[widest] + 1) % array.shape[widest]] + place[widest + 1:]
    return array.at[tuple(place)].set(least).at[tuple(neighbour)].set(high)


def steps_of(rng, dims, cuts, low, top_value):
    level = 1.0
    for dim, shards_of in cuts:
        draws = jax.random.uniform(jax.random.fold_in(jax.random.fold_in(rng, 6), dim), (shards_of,), jnp.float32, low / len(cuts), top_value / len(cuts))
        level = level * jnp.repeat(jnp.exp(draws), dims[dim] // shards_of).reshape((-1,) + (1,) * (len(dims) - 1 - dim))
    return level


def gaussian(own_key, shape, scale, reach, cuts=(), kind=jnp.bfloat16):
    drawn = jax.random.normal(own_key, shape, jnp.float32) * scale
    if len(cuts) > 0:
        drawn = steps_of(own_key, shape, cuts, -0.22, 0.18) * drawn
    return jnp.clip(drawn, min=-reach, max=reach).astype(kind)


def setup_inputs(seed: int = 0) -> dict:
    streams_of = jax.random.split(jax.random.key(seed), 9)
    queries = draw_queries(jax.random.fold_in(streams_of[8], 71), 0)
    key_rows = draw_key_rows(jax.random.fold_in(streams_of[8], 71), 0)
    value_rows = gaussian(streams_of[2], (TOKENS, D), 1.0, 6.0, ((0, 32), (1, 8)))
    neighbours = draw_neighbours(jax.random.fold_in(streams_of[8], 71), 0)
    tile_counts = draw_tile_counts(jax.random.fold_in(streams_of[8], 71), 0)
    panels = gaussian(streams_of[5], (TOKENS, SECTIONS * D), 0.2, 3.0, ((0, 32), (1, 8)))
    alignment = gaussian(streams_of[6], (D, D), HDIM ** -0.5, 0.5, ((0, 8),))
    tap_pick = with_ends(jax.random.randint(streams_of[7], (TILES,), 0, SECTIONS), jax.random.fold_in(streams_of[7], 1), 0, SECTIONS - 1).astype(jnp.int32)
    return {"queries": queries, "key_rows": key_rows, "value_rows": value_rows, "neighbours": neighbours, "tile_counts": tile_counts, "panels": panels, "alignment": alignment, "tap_pick": tap_pick}


def reference(queries, key_rows, value_rows, neighbours, tile_counts, panels, alignment, tap_pick):
    query_tiles = queries.reshape(TILES, TILE, HEADS, HDIM)
    key_tiles = key_rows.reshape(TILES, TILE, HEADS, HDIM)
    value_tiles = value_rows.reshape(TILES, TILE, HEADS, HDIM)
    slot_of = jnp.arange(NB * TILE, dtype=jnp.int32) // TILE

    def one_tile(index):
        near_ids = neighbours[index]
        near_keys = key_tiles[near_ids].reshape(NB * TILE, HEADS, HDIM).astype(jnp.float32)
        near_values = value_tiles[near_ids].reshape(NB * TILE, HEADS, HDIM).astype(jnp.float32)
        scores = jnp.einsum("qhd,khd->hqk", query_tiles[index].astype(jnp.float32), near_keys) * (HDIM ** -0.5)
        is_live = slot_of < tile_counts[index]
        scores = jnp.where(is_live[None, None, :], scores, -jnp.inf)
        row_max = jnp.max(scores, axis=-1, keepdims=True)
        exp_terms = jnp.exp(scores - row_max)
        weights = (exp_terms / jnp.sum(exp_terms, axis=-1, keepdims=True)).astype(jnp.bfloat16)
        result = jnp.einsum("hqk,khd->qhd", weights.astype(jnp.float32), near_values)
        return result.astype(jnp.bfloat16)

    attended = lax.map(one_tile, jnp.arange(TILES, dtype=jnp.int32)).reshape(TOKENS, HEADS * HDIM)
    width = HEADS * HDIM
    col_share = width // GROUPS
    row_pick = jnp.repeat(tap_pick.astype(jnp.int32), TILE)
    total = jnp.zeros((TOKENS, width), jnp.float32)
    for group in range(GROUPS):
        block = panels[:, group * PANEL_COLS:(group + 1) * PANEL_COLS]
        padded = jnp.pad(block, ((0, 0), (width, width)))
        target = jnp.zeros((TOKENS, width), jnp.bfloat16)
        for section in range(SECTIONS):
            start = min(max(section * width - group * PANEL_COLS + width, 0), PANEL_COLS + width)
            candidate = padded[:, start:start + width]
            target = jnp.where((row_pick == section)[:, None], candidate, target)
        partial_value = jnp.dot(attended[:, group * col_share:(group + 1) * col_share],
                          alignment[group * col_share:(group + 1) * col_share, :],
                          preferred_element_type=jnp.float32)
        total = total + (partial_value - target.astype(jnp.float32))
    residual = total.astype(jnp.bfloat16)
    grad_align = jnp.dot(attended.T, residual, preferred_element_type=jnp.float32)
    grad_attn = jnp.dot(residual, alignment.T, preferred_element_type=jnp.float32).astype(jnp.bfloat16)
    return grad_align, grad_attn
```

```python
import functools

import jax
import jax.numpy as jnp
import numpy as np
from jax import lax
from jax.experimental import pallas as pl
from jax.experimental.pallas import tpu as pltpu
from jax.sharding import Mesh, PartitionSpec as P

HDIM = 128
TILE = 384
NB = 4
LOG2E = 1.4426950408889634
F32 = jnp.float32
BF16 = jnp.bfloat16
SEQ = ("zl", "y", "c")
SEG = ("zh", "x")


def shift(a, axis, d):
    n = lax.axis_size(axis)
    return lax.ppermute(a, axis, [(i, (i + d) % n) for i in range(n)])


def attn_kernel(meta, q_ref, kp, ko, kn, vp, vo, vn, out_ref, kbuf, vbuf, scores, ksem, vsem):
    heads = q_ref.shape[1] // HDIM
    count = meta[1]

    def fetch(j, parts, buf, sem):
        tile = meta[2 + j]
        for part, ref in enumerate(parts):
            @pl.when(tile // 2 == part)
            def _():
                rows = pl.ds(pl.multiple_of((tile - 2 * part) * TILE, TILE), TILE)
                pltpu.make_async_copy(ref.at[rows], buf.at[j], sem.at[j]).start()

    for j in range(NB):
        fetch(j, (kp, ko, kn), kbuf, ksem)
    for j in range(NB):
        fetch(j, (vp, vo, vn), vbuf, vsem)
    for j in range(NB):
        pltpu.make_async_copy(ko.at[pl.ds(0, TILE)], kbuf.at[j], ksem.at[j]).wait()
    for j in range(NB):
        pltpu.make_async_copy(vo.at[pl.ds(0, TILE)], vbuf.at[j], vsem.at[j]).wait()
    factor = HDIM ** (-0.5) * LOG2E
    for h in range(heads):
        cols = slice(h * HDIM, (h + 1) * HDIM)
        q = q_ref[:, cols]
        top = None
        for j in range(NB):
            s = lax.dot_general(q, kbuf[j, :, cols], (((1,), (1,)), ((), ())), preferred_element_type=F32)
            if j >= 2:
                s = jnp.where(j < count, s, -jnp.inf)
            scores[:, j * TILE:(j + 1) * TILE] = s
            m = jnp.max(s, axis=1, keepdims=True)
            top = m if top is None else jnp.maximum(top, m)
        total = None
        acc = None
        for j in range(NB):
            e = jnp.exp2((scores[:, j * TILE:(j + 1) * TILE] - top) * factor)
            part = jnp.sum(e, axis=1, keepdims=True)
            total = part if total is None else total + part
            o = jnp.dot(e.astype(BF16), vbuf[j, :, cols], preferred_element_type=F32)
            acc = o if acc is None else acc + o
        out_ref[:, cols] = (acc / total).astype(BF16)


def tile_attention(meta, queries, halo_k, halo_v):
    width = queries.shape[1]
    grid_spec = pltpu.PrefetchScalarGridSpec(
        num_scalar_prefetch=1,
        grid=(1,),
        in_specs=[pl.BlockSpec((TILE, width), lambda i, meta: (meta[0], 0))]
        + [pl.BlockSpec(memory_space=pl.ANY)] * 6,
        out_specs=pl.BlockSpec((TILE, width), lambda i, meta: (0, 0)),
        scratch_shapes=[
            pltpu.VMEM((NB, TILE, width), BF16),
            pltpu.VMEM((NB, TILE, width), BF16),
            pltpu.VMEM((TILE, NB * TILE), F32),
            pltpu.SemaphoreType.DMA((NB,)),
            pltpu.SemaphoreType.DMA((NB,)),
        ],
    )
    flops = 4 * TILE * NB * TILE * width
    return pl.pallas_call(
        attn_kernel,
        grid_spec=grid_spec,
        out_shape=jax.ShapeDtypeStruct((TILE, width), BF16),
        compiler_params=pltpu.CompilerParams(vmem_limit_bytes=40 * 2**20),
        cost_estimate=pl.CostEstimate(flops=flops, bytes_accessed=4 * 2**20, transcendentals=3 * NB * TILE * TILE),
        name="tile_attention",
    )(meta, queries, *halo_k, *halo_v)


def grads_kernel(meta, *refs):
    atts = refs[:8]
    parts, target, ga_other, ga_keep, p_own, p_oth, abuf, sem = refs[8:]
    col_flip, core, y, zh, x = meta[0], meta[1], meta[2], meta[3], meta[4]
    step = parts.shape[3]

    def copies():
        for part in range(8):
            for rel in range(2):
                off = pl.multiple_of(jnp.bitwise_xor(col_flip, rel) * TILE, TILE)
                yield pltpu.make_async_copy(
                    parts.at[part, rel],
                    abuf.at[:, pl.ds(part * step, step), pl.ds(off, TILE)],
                    sem.at[part, rel],
                )

    for copy in copies():
        copy.start()
    for copy in copies():
        copy.wait()
    acc = -target[...].astype(F32)
    for j in range(8):
        acc = acc + jnp.dot(atts[j][...], abuf[j], preferred_element_type=F32)
    residual = acc.astype(BF16)
    halves = (residual[:, :TILE], residual[:, TILE:])
    swap = core == 1
    r_keep = jnp.where(swap, halves[1], halves[0])
    r_other = jnp.where(swap, halves[0], halves[1])
    for r, out in ((r_other, ga_other), (r_keep, ga_keep)):
        r_t = r.T
        for j in range(8):
            g = jnp.bitwise_xor(zh, j // 4) * 4 + lax.rem(x + j % 4, 4)
            val = jnp.dot(r_t, atts[j][...], preferred_element_type=F32).astype(BF16)
            for k in range(4):
                out[lax.rem(k + 4 - y, 4), g] = val[96 * k:96 * (k + 1)]
    for j in range(8):
        val = lax.dot_general(residual, abuf[j], (((1,), (1,)), ((), ())), preferred_element_type=F32)
        (p_own if j < 4 else p_oth)[j % 4] = val.astype(BF16)


def gradients(meta, atts, parts, target):
    vmem = pl.BlockSpec(memory_space=pltpu.VMEM)
    return pl.pallas_call(
        grads_kernel,
        in_specs=[pl.BlockSpec(memory_space=pltpu.SMEM)] + [vmem] * 8 + [pl.BlockSpec(memory_space=pl.ANY), vmem],
        out_specs=[vmem] * 4,
        out_shape=[
            jax.ShapeDtypeStruct((4, 8, 96, TILE), BF16),
            jax.ShapeDtypeStruct((4, 8, 96, TILE), BF16),
            jax.ShapeDtypeStruct((4, TILE, TILE), BF16),
            jax.ShapeDtypeStruct((4, TILE, TILE), BF16),
        ],
        scratch_shapes=[pltpu.VMEM((8, TILE, 2 * TILE), BF16), pltpu.SemaphoreType.DMA((8, 2))],
        compiler_params=pltpu.CompilerParams(vmem_limit_bytes=48 * 2**20),
        cost_estimate=pl.CostEstimate(flops=6 * TILE * 3072 * 768, bytes_accessed=20 * 2**20, transcendentals=0),
        name="gradients",
    )(meta, *atts, parts, target)


def block_of(x):
    return 2 * (x % 2) + x // 2


def alignment_parts(alignment, x, zl, y, c):
    rows = lax.dynamic_slice_in_dim(alignment, 48 * (2 * y + c), 48, 0)
    pieces = []
    for e in range(4):
        dest = (x + 4 - e) % 4
        piece = lax.dynamic_slice_in_dim(rows, 768 * block_of(dest) + TILE * (zl % 2), TILE, 1)
        pieces.append(shift(piece, "x", -e) if e else piece)
    own = jnp.stack(pieces)
    both = jnp.concatenate([own, shift(own, "zh", 1)])
    paired = lax.ppermute(both, "zl", [(i, i ^ 1) for i in range(4)])
    return lax.all_gather(jnp.stack([both, paired]), ("y", "c"))


def own_target(panels, tap_pick, zh, x):
    p = x // 2
    width = panels.shape[1] // 2
    tiles = panels.reshape(2, TILE, 2 * width)
    picks = []
    for rel in (1, 0):
        tile = zh ^ rel
        rows = lax.dynamic_index_in_dim(tiles, tile, 0, keepdims=False)
        keep = lax.dynamic_slice_in_dim(rows, p * width, width, 1)
        give = lax.dynamic_slice_in_dim(rows, (1 - p) * width, width, 1)
        got = shift(give, "x", 2)
        tap = lax.dynamic_index_in_dim(tap_pick, tile, 0, keepdims=False)
        picks.append(jnp.where(tap % 2 == p, keep, got))
    got = shift(picks[0], "zh", 1)
    tap = lax.dynamic_index_in_dim(tap_pick, zh, 0, keepdims=False)
    return jnp.where(tap // 2 == zh, picks[1], got)


def on_device(queries, key_rows, value_rows, neighbours, tile_counts, panels, alignment, tap_pick):
    zh, x, zl, y, c = (lax.axis_index(name) for name in ("zh", "x", "zl", "y", "c"))
    seq = (zl * 4 + y) * 2 + c
    count = 32
    up = [(i, i + 1) for i in range(count - 1)]
    down = [(i + 1, i) for i in range(count - 1)]
    halo_k = (lax.ppermute(key_rows, SEQ, up), key_rows, lax.ppermute(key_rows, SEQ, down))
    halo_v = (lax.ppermute(value_rows, SEQ, up), value_rows, lax.ppermute(value_rows, SEQ, down))
    local_ids = neighbours - (seq - 1) * 2

    def attend(tile):
        meta = jnp.concatenate([
            tile.reshape(1),
            lax.dynamic_slice_in_dim(tile_counts, tile, 1),
            lax.dynamic_slice_in_dim(local_ids, tile, 1, 0).reshape(NB),
        ]).astype(jnp.int32)
        return tile_attention(meta, queries, halo_k, halo_v)

    parts = alignment_parts(alignment, x, zl, y, c)
    target = own_target(panels, tap_pick, zh, x)
    att_send = attend(1 - zh)
    att_keep = attend(zh)
    att_got = shift(att_send, "zh", 1)
    atts = [att_keep] + [shift(att_keep, "x", -e) for e in (1, 2, 3)]
    atts += [att_got] + [shift(att_got, "x", -e) for e in (1, 2, 3)]
    meta = jnp.stack([zl % 2, c, y, zh, x]).astype(jnp.int32)
    ga_other, ga_keep, p_own, p_oth = gradients(meta, atts, parts, target)

    def x_sum(pieces):
        total = pieces[0].astype(F32)
        for e in (1, 2, 3):
            total = total + shift(pieces[e], "x", e).astype(F32)
        return total.astype(BF16)

    attn_away = shift(x_sum(p_oth), "zh", 1)
    attn_here = x_sum(p_own)
    grad_attn = jnp.concatenate([
        jnp.where(zh == 0, attn_here, attn_away),
        jnp.where(zh == 0, attn_away, attn_here),
    ])

    pair = (ga_keep.astype(F32) + shift(ga_other, "c", 1).astype(F32)).astype(BF16)
    total = pair[0].astype(F32)
    for d in (1, 2, 3):
        total = total + shift(pair[d], "y", d).astype(F32)
    exchanged = lax.all_to_all(total.astype(BF16), ("zh", "zl"), 0, 0)
    block = jnp.sum(exchanged.astype(F32), axis=0)
    sizes = (2, 4, 4, 4, 2)
    moves = []
    for index in range(256):
        h, i, l, j, k = (int(n) for n in np.unravel_index(index, sizes))
        dest = (h, l, block_of(i), 2 * k + j // 2, j % 2)
        moves.append((index, int(np.ravel_multi_index(dest, sizes))))
    grad_align = lax.ppermute(block, SEG + SEQ, moves).T
    return grad_align, grad_attn


def solution(mesh):
    fine = Mesh(mesh.devices.reshape(2, 4, 4, 4, 2), SEG + SEQ)
    placed = (
        P(SEQ, SEG),
        P(SEQ, SEG),
        P(SEQ, SEG),
        P(SEQ, None),
        P(SEQ),
        P(SEQ, SEG),
        P(SEG, None),
        P(SEQ),
    )
    return jax.shard_map(
        on_device,
        mesh=fine,
        in_specs=placed,
        out_specs=(P(SEG, SEQ), P(SEQ, SEG)),
        check_vma=False,
    )
```

```python
import jax
import jax.numpy as jnp
import numpy as np
from jax import lax
from jax.experimental import pallas as pl
from jax.experimental.pallas import tpu as pltpu
from jax.sharding import Mesh, PartitionSpec as P

HDIM = 128
TILE = 384
NB = 4
LOG2E = 1.4426950408889634
F32 = jnp.float32
BF16 = jnp.bfloat16
SEQ = ("zl", "y", "c")
SEG = ("zh", "x")


def shift(a, axis, d):
    n = lax.axis_size(axis)
    return lax.ppermute(a, axis, [(i, (i + d) % n) for i in range(n)])


def after(value, *earlier):
    return lax.optimization_barrier((value, *earlier))[0]


def attn_kernel(meta, q_ref, before, here, after, out_ref, kvbuf, scores, sem):
    width = q_ref.shape[1]
    heads = width // HDIM
    count = meta[1]
    for half in range(2):
        cols = pl.ds(half * width, width)
        for j in range(NB):
            tile = meta[2 + j]
            for part, ref in enumerate((before, here, after)):
                @pl.when(tile // 2 == part)
                def _():
                    rows = pl.ds(pl.multiple_of((tile - 2 * part) * TILE, TILE), TILE)
                    pltpu.make_async_copy(ref.at[rows, cols], kvbuf.at[half, j], sem.at[half, j]).start()

    def arrive(half):
        for j in range(NB):
            cols = pl.ds(half * width, width)
            pltpu.make_async_copy(here.at[pl.ds(0, TILE), cols], kvbuf.at[half, j], sem.at[half, j]).wait()

    arrive(0)
    arrive(1)
    factor = HDIM ** (-0.5) * LOG2E
    for h in range(heads):
        cols = slice(h * HDIM, (h + 1) * HDIM)
        q = q_ref[:, cols]
        top = None
        for j in range(NB):
            s = lax.dot_general(q, kvbuf[0, j, :, cols], (((1,), (1,)), ((), ())), preferred_element_type=F32)
            if j >= 2:
                s = jnp.where(j < count, s, -jnp.inf)
            scores[:, j * TILE:(j + 1) * TILE] = s
            m = jnp.max(s, axis=1, keepdims=True)
            top = m if top is None else jnp.maximum(top, m)
        total = None
        acc = None
        for j in range(NB):
            e = jnp.exp2((scores[:, j * TILE:(j + 1) * TILE] - top) * factor)
            part = jnp.sum(e, axis=1, keepdims=True)
            total = part if total is None else total + part
            o = jnp.dot(e.astype(BF16), kvbuf[1, j, :, cols], preferred_element_type=F32)
            acc = o if acc is None else acc + o
        out_ref[:, cols] = (acc / total).astype(BF16)


def tile_attention(meta, queries, halo):
    width = queries.shape[1]
    grid_spec = pltpu.PrefetchScalarGridSpec(
        num_scalar_prefetch=1,
        grid=(1,),
        in_specs=[pl.BlockSpec((TILE, width), lambda i, meta: (meta[0], 0))]
        + [pl.BlockSpec(memory_space=pl.ANY)] * 3,
        out_specs=pl.BlockSpec((TILE, width), lambda i, meta: (0, 0)),
        scratch_shapes=[
            pltpu.VMEM((2, NB, TILE, width), BF16),
            pltpu.VMEM((TILE, NB * TILE), F32),
            pltpu.SemaphoreType.DMA((2, NB)),
        ],
    )
    return pl.pallas_call(
        attn_kernel,
        grid_spec=grid_spec,
        out_shape=jax.ShapeDtypeStruct((TILE, width), BF16),
        compiler_params=pltpu.CompilerParams(vmem_limit_bytes=40 * 2**20),
        cost_estimate=pl.CostEstimate(
            flops=4 * TILE * NB * TILE * width, bytes_accessed=4 * 2**20, transcendentals=3 * NB * TILE * TILE
        ),
        name="tile_attention",
    )(meta, queries, *halo)


def fetch_all(copies):
    for copy in copies:
        copy.start()
    return copies


def wait_all(copies):
    for copy in copies:
        copy.wait()


def part_copies(meta, parts, abuf, sem):
    step = parts[0].shape[2]
    copies = []
    for n, ref in enumerate(parts):
        row = 2 * lax.rem(meta[0] + n // 2, 4) + jnp.bitwise_xor(meta[1], n % 2)
        rows = pl.ds(pl.multiple_of(row * step, step), step)
        copies.append(pltpu.make_async_copy(ref, abuf.at[:, :, rows, :], sem.at[n]))
    return copies


def group_of(meta, j):
    return jnp.bitwise_xor(meta[2], j // 4) * 4 + lax.rem(meta[3] + j % 4, 4)


def transposed_product(meta, r, atts, write):
    r_t = r.T
    for j in range(8):
        val = jnp.dot(r_t, atts[j], preferred_element_type=F32)
        for k in range(4):
            write(lax.rem(k + 4 - meta[0], 4), group_of(meta, j), val[96 * k:96 * (k + 1)])


def residual_kernel(meta, *refs):
    atts, parts = refs[:8], refs[8:16]
    target, res_ref, away_ref, abuf, attbuf, sem, att_sem = refs[16:]
    loads = fetch_all([pltpu.make_async_copy(atts[j], attbuf.at[j], att_sem.at[j]) for j in range(8)])
    loads += fetch_all(part_copies(meta, parts, abuf, sem))
    wait_all(loads)
    for half in range(2):
        cols = slice(half * TILE, (half + 1) * TILE)
        acc = -target[:, cols].astype(F32)
        for j in range(8):
            acc = acc + jnp.dot(attbuf[j], abuf[j % 4, j // 4, :, cols], preferred_element_type=F32)
        res_ref[half] = acc.astype(BF16)

    def write(d, g, val):
        away_ref[d, g] = val.astype(BF16)

    transposed_product(meta, res_ref[1 - meta[1]], attbuf, write)


def attn_grad_kernel(meta, *refs):
    res_ref, parts = refs[0], refs[1:9]
    outs, abuf, sem = refs[9:17], refs[17], refs[18]
    wait_all(fetch_all(part_copies(meta, parts, abuf, sem)))
    contract = (((1,), (1,)), ((), ()))
    for j in (4, 5, 6, 7, 0, 1, 2, 3):
        val = lax.dot_general(res_ref[0], abuf[j % 4, j // 4, :, :TILE], contract, preferred_element_type=F32)
        val = val + lax.dot_general(
            res_ref[1], abuf[j % 4, j // 4, :, TILE:], contract, preferred_element_type=F32
        )
        outs[j][...] = val.astype(BF16)


def align_grad_kernel(meta, *refs):
    res_ref, atts, arrived = refs[0], refs[1:9], refs[9]
    here, right, left, far_right, far_left, pairs, attbuf, got, sem = refs[11:]
    loads = fetch_all([pltpu.make_async_copy(atts[j], attbuf.at[j], sem.at[j]) for j in range(8)])
    loads += fetch_all([pltpu.make_async_copy(arrived, got, sem.at[8])])
    wait_all(loads)

    def write(d, g, val):
        pairs[d, g] = (val + got[d, g].astype(F32)).astype(BF16)

    transposed_product(meta, res_ref[meta[1]], attbuf, write)
    here[...] = pairs[0]
    right[...] = pairs[1]
    far_right[...] = pairs[2, :4]
    far_left[...] = pairs[2, 4:]
    left[...] = pairs[3]


def add_far_kernel(right, left, from_left, from_right, right_out, left_out):
    right_out[4:] = right[4:]
    right_out[:4] = (right[:4].astype(F32) + from_left[...].astype(F32)).astype(BF16)
    left_out[:4] = left[:4]
    left_out[4:] = (left[4:].astype(F32) + from_right[...].astype(F32)).astype(BF16)


SMEM = pl.BlockSpec(memory_space=pltpu.SMEM)
VMEM = pl.BlockSpec(memory_space=pltpu.VMEM)
ANY = pl.BlockSpec(memory_space=pl.ANY)
FLOPS = 2 * TILE * 3072 * 768


def x_sum(pieces):
    total = pieces[0].astype(F32)
    for e in (1, 2, 3):
        total = total + shift(pieces[e], "x", e).astype(F32)
    return total.astype(BF16)


def gradients(meta, atts, parts, target):
    params = pltpu.CompilerParams(vmem_limit_bytes=40 * 2**20)
    abuf = pltpu.VMEM((4, 2, TILE, 2 * TILE), BF16)
    attbuf = pltpu.VMEM((8, TILE, TILE), BF16)
    pieces = jax.ShapeDtypeStruct((4, 8, 96, TILE), BF16)
    residual, away = pl.pallas_call(
        residual_kernel,
        in_specs=[SMEM] + [ANY] * 16 + [VMEM],
        out_specs=[VMEM] * 2,
        out_shape=[jax.ShapeDtypeStruct((2, TILE, TILE), BF16), pieces],
        scratch_shapes=[abuf, attbuf, pltpu.SemaphoreType.DMA((8,)), pltpu.SemaphoreType.DMA((8,))],
        compiler_params=params,
        cost_estimate=pl.CostEstimate(flops=2 * FLOPS, bytes_accessed=10 * 2**20, transcendentals=0),
        name="residual",
    )(meta, *atts, *parts, target)
    arrived = shift(away, "c", 1)
    partials = pl.pallas_call(
        attn_grad_kernel,
        in_specs=[SMEM, VMEM] + [ANY] * 8,
        out_specs=[VMEM] * 8,
        out_shape=[jax.ShapeDtypeStruct((TILE, TILE), BF16)] * 8,
        scratch_shapes=[abuf, pltpu.SemaphoreType.DMA((8,))],
        compiler_params=params,
        cost_estimate=pl.CostEstimate(flops=FLOPS, bytes_accessed=8 * 2**20, transcendentals=0),
        name="attn_grad_terms",
    )(meta, residual, *parts)
    half_piece = jax.ShapeDtypeStruct((4, 96, TILE), BF16)
    whole_piece = jax.ShapeDtypeStruct((8, 96, TILE), BF16)
    here, right, left, far_right, far_left = pl.pallas_call(
        align_grad_kernel,
        in_specs=[SMEM, VMEM] + [ANY] * 10,
        out_specs=[VMEM] * 5,
        out_shape=[whole_piece] * 3 + [half_piece] * 2,
        scratch_shapes=[
            pltpu.VMEM((4, 8, 96, TILE), BF16),
            attbuf,
            pltpu.VMEM((4, 8, 96, TILE), BF16),
            pltpu.SemaphoreType.DMA((9,)),
        ],
        compiler_params=params,
        cost_estimate=pl.CostEstimate(flops=FLOPS, bytes_accessed=8 * 2**20, transcendentals=0),
        name="align_grad_terms",
    )(meta, residual, *atts, arrived, partials[0])
    attn_away = x_sum(partials[4:])
    right = after(right, attn_away)
    right, left = pl.pallas_call(
        add_far_kernel,
        in_specs=[VMEM] * 4,
        out_specs=[VMEM] * 2,
        out_shape=[whole_piece] * 2,
        compiler_params=params,
        cost_estimate=pl.CostEstimate(flops=0, bytes_accessed=4 * 2**20, transcendentals=0),
        name="add_far",
    )(right, left, shift(far_right, "y", 1), shift(far_left, "y", -1))
    total = here.astype(F32) + shift(right, "y", 1).astype(F32) + shift(left, "y", -1).astype(F32)
    return partials[:4], attn_away, total.astype(BF16)


def block_of(x):
    return 2 * (x % 2) + x // 2


def copy_all_kernel(meta, plan, *refs):
    count = len(refs) - 1
    sem = refs[count]
    loads = [pltpu.make_async_copy(src, dst, sem.at[n]) for n, (src, dst) in enumerate(plan(meta, refs[:count]))]
    wait_all(fetch_all(loads))


def copy_all(meta, plan, copies, arrays, outs, name):
    return pl.pallas_call(
        lambda meta_ref, *refs: copy_all_kernel(meta_ref, plan, *refs),
        in_specs=[SMEM] + [ANY] * len(arrays),
        out_specs=[ANY] * len(outs),
        out_shape=[jax.ShapeDtypeStruct(shape, BF16) for shape in outs],
        scratch_shapes=[pltpu.SemaphoreType.DMA((copies,))],
        compiler_params=pltpu.CompilerParams(vmem_limit_bytes=16 * 2**20),
        name=name,
    )(meta, *arrays)


def first_copies(meta, key_rows, value_rows, alignment, panels):
    tokens, width = key_rows.shape
    model = alignment.shape[1]
    block = panels.shape[1] // 2

    def plan(meta, refs):
        k, v, a, p, both, rows, give = refs
        return [
            (a.at[pl.ds(pl.multiple_of(meta[0] * 48, 48), 48)], rows),
            (k, both.at[:, pl.ds(0, width)]),
            (v, both.at[:, pl.ds(width, width)]),
            (p.at[pl.ds(pl.multiple_of(meta[1] * TILE, TILE), TILE),
                  pl.ds(pl.multiple_of(meta[2] * block, block), block)], give),
        ]

    outs = [(tokens, 2 * width), (48, model), (TILE, block)]
    return copy_all(meta, plan, 4, (key_rows, value_rows, alignment, panels), outs, "first_copies")


def alignment_parts(rows, halo, arrived, x):
    width = rows.shape[1] // 4
    got_rows = after(shift(rows, "zh", 1), halo[0], halo[2])
    blocks = jnp.stack([block_of(lax.rem(x + 4 - e, 4)) for e in range(4)]).astype(jnp.int32)

    def plan(meta, refs):
        own, got = refs[:2]
        pairs = []
        for e in range(4):
            cols = pl.ds(pl.multiple_of(meta[e] * width, width), width)
            pairs += [(own.at[:, cols], refs[2 + e].at[0]), (got.at[:, cols], refs[2 + e].at[1])]
        return pairs

    pieces = copy_all(blocks, plan, 8, (rows, got_rows), [(2, 48, width)] * 4, "alignment_cut")
    own = jnp.stack([shift(pieces[e], "x", -e) if e else pieces[0] for e in range(4)])
    parts = []
    for d in range(4):
        got = shift(own, "y", -d) if d else own
        parts += [got, shift(after(got, arrived) if d == 2 else got, "c", 1)]
    return parts


def own_pick(panels, tap_pick, give, tile, p):
    width = panels.shape[1] // 2
    rows = lax.dynamic_slice(panels, (tile * TILE, p * width), (TILE, width))
    got = shift(give, "x", 2)
    tap = lax.dynamic_index_in_dim(tap_pick, tile, 0, keepdims=False)
    return jnp.where((tap & 1) == p, rows, got), got


def on_device(queries, key_rows, value_rows, neighbours, tile_counts, panels, alignment, tap_pick):
    zh, x, zl, y, c = (lax.axis_index(name) for name in ("zh", "x", "zl", "y", "c"))
    seq = (zl * 4 + y) * 2 + c
    count = 32
    up = [(i, i + 1) for i in range(count - 1)]
    down = [(i + 1, i) for i in range(count - 1)]
    p = x // 2
    start = jnp.stack([2 * y + c, 1 - zh, 1 - p]).astype(jnp.int32)
    both, rows, give = first_copies(start, key_rows, value_rows, alignment, panels)
    halo = (lax.ppermute(both, SEQ, up), both, lax.ppermute(both, SEQ, down))
    local_ids = neighbours - (seq - 1) * 2

    def attend(tile):
        meta = jnp.concatenate([
            tile.reshape(1),
            lax.dynamic_slice_in_dim(tile_counts, tile, 1),
            lax.dynamic_slice_in_dim(local_ids, tile, 1, 0).reshape(NB),
        ]).astype(jnp.int32)
        return tile_attention(meta, queries, halo)

    pick_away, got = own_pick(panels, tap_pick, give, 1 - zh, p)
    later_p = after(p, got)
    width = panels.shape[1] // 2
    give = lax.dynamic_slice(panels, (zh * TILE, (1 - later_p) * width), (TILE, width))
    pick_here, _ = own_pick(panels, tap_pick, give, zh, p)
    att_send = attend(1 - zh)
    att_got = shift(att_send, "zh", 1)
    att_keep = attend(zh)
    arrived = shift(after(pick_away, att_send), "zh", 1)
    parts = alignment_parts(rows, halo, arrived, x)
    tap = lax.dynamic_index_in_dim(tap_pick, zh, 0, keepdims=False)
    target = jnp.where(tap // 2 == zh, pick_here, arrived)
    atts = [att_keep] + [shift(att_keep, "x", -e) for e in (1, 2, 3)]
    atts += [att_got] + [shift(att_got, "x", -e) for e in (1, 2, 3)]
    meta = jnp.stack([y, c, zh, x]).astype(jnp.int32)
    partials, attn_away, total = gradients(meta, atts, parts, target)

    attn_away = shift(attn_away, "zh", 1)
    attn_here = x_sum(partials)
    grad_attn = jnp.concatenate([
        jnp.where(zh == 0, attn_here, attn_away),
        jnp.where(zh == 0, attn_away, attn_here),
    ])

    exchanged = lax.all_to_all(after(total, attn_away, attn_here), ("zh", "zl"), 0, 0)
    block = jnp.sum(exchanged.astype(F32), axis=0).astype(BF16)
    sizes = (2, 4, 4, 4, 2)
    moves = []
    for index in range(256):
        h, i, l, j, k = (int(n) for n in np.unravel_index(index, sizes))
        dest = (h, l, block_of(i), 2 * k + j // 2, j % 2)
        moves.append((index, int(np.ravel_multi_index(dest, sizes))))
    grad_align = lax.ppermute(block, SEG + SEQ, moves).T.astype(F32)
    return grad_align, grad_attn


def solution(mesh):
    fine = Mesh(mesh.devices.reshape(2, 4, 4, 4, 2), SEG + SEQ)
    placed = (
        P(SEQ, SEG),
        P(SEQ, SEG),
        P(SEQ, SEG),
        P(SEQ, None),
        P(SEQ),
        P(SEQ, SEG),
        P(SEG, None),
        P(SEQ),
    )
    return jax.shard_map(
        on_device,
        mesh=fine,
        in_specs=placed,
        out_specs=(P(SEG, SEQ), P(SEQ, SEG)),
        check_vma=False,
    )
```

```python
import jax
import jax.numpy as jnp
import numpy as np
from jax import lax
from jax.experimental import pallas as pl
from jax.experimental.pallas import tpu as pltpu
from jax.sharding import Mesh, PartitionSpec as P

HDIM = 128
TILE = 384
NB = 4
LOG2E = 1.4426950408889634
F32 = jnp.float32
BF16 = jnp.bfloat16
SEQ = ("zl", "y", "c")
SEG = ("zh", "x")
SMALL = pl.CostEstimate(flops=1, bytes_accessed=1, transcendentals=0)
PARAMS = pltpu.CompilerParams(vmem_limit_bytes=24 * 2**20)


def shift(a, axis, d):
    n = lax.axis_size(axis)
    return lax.ppermute(a, axis, [(i, (i + d) % n) for i in range(n)])


def after(value, *earlier):
    return lax.optimization_barrier((value, *earlier))[0]


def attn_kernel(meta, q_ref, before, here, after, out_ref, kvbuf, scores, sem):
    width = q_ref.shape[1]
    heads = width // HDIM
    count = meta[1]
    for half in range(2):
        cols = pl.ds(half * width, width)
        for j in range(NB):
            tile = meta[2 + j]
            for part, ref in enumerate((before, here, after)):
                @pl.when(tile // 2 == part)
                def _():
                    rows = pl.ds(pl.multiple_of((tile - 2 * part) * TILE, TILE), TILE)
                    pltpu.make_async_copy(ref.at[rows, cols], kvbuf.at[half, j], sem.at[half, j]).start()

    def arrive(half):
        for j in range(NB):
            cols = pl.ds(half * width, width)
            pltpu.make_async_copy(here.at[pl.ds(0, TILE), cols], kvbuf.at[half, j], sem.at[half, j]).wait()

    arrive(0)
    arrive(1)
    factor = HDIM ** (-0.5) * LOG2E
    for h in range(heads):
        cols = slice(h * HDIM, (h + 1) * HDIM)
        q = q_ref[:, cols]
        top = None
        for j in range(NB):
            s = lax.dot_general(q, kvbuf[0, j, :, cols], (((1,), (1,)), ((), ())), preferred_element_type=F32)
            if j >= 2:
                s = jnp.where(j < count, s, -jnp.inf)
            scores[:, j * TILE:(j + 1) * TILE] = s
            m = jnp.max(s, axis=1, keepdims=True)
            top = m if top is None else jnp.maximum(top, m)
        total = None
        acc = None
        for j in range(NB):
            e = jnp.exp2((scores[:, j * TILE:(j + 1) * TILE] - top) * factor)
            part = jnp.sum(e, axis=1, keepdims=True)
            total = part if total is None else total + part
            o = jnp.dot(e.astype(BF16), kvbuf[1, j, :, cols], preferred_element_type=F32)
            acc = o if acc is None else acc + o
        out_ref[:, cols] = (acc / total).astype(BF16)


def tile_attention(meta, queries, halo):
    width = queries.shape[1]
    grid_spec = pltpu.PrefetchScalarGridSpec(
        num_scalar_prefetch=1,
        grid=(1,),
        in_specs=[pl.BlockSpec((TILE, width), lambda i, meta: (meta[0], 0))]
        + [pl.BlockSpec(memory_space=pl.ANY)] * 3,
        out_specs=pl.BlockSpec((TILE, width), lambda i, meta: (0, 0)),
        scratch_shapes=[
            pltpu.VMEM((2, NB, TILE, width), BF16),
            pltpu.VMEM((TILE, NB * TILE), F32),
            pltpu.SemaphoreType.DMA((2, NB)),
        ],
    )
    return pl.pallas_call(
        attn_kernel,
        grid_spec=grid_spec,
        out_shape=jax.ShapeDtypeStruct((TILE, width), BF16),
        compiler_params=PARAMS,
        cost_estimate=SMALL,
        name="tile_attention",
    )(meta, queries, *halo)


def fetch_all(copies):
    for copy in copies:
        copy.start()
    return copies


def wait_all(copies):
    for copy in copies:
        copy.wait()


def part_copies(meta, parts, abuf, sem, cols, e):
    copies = []
    for n, ref in enumerate(parts):
        step = ref.shape[2]
        rows = pl.ds(pl.multiple_of(jnp.bitwise_xor(meta[1], n) * step, step), step)
        copies.append(pltpu.make_async_copy(ref.at[e, :, :, cols], abuf.at[e, :, rows, :], sem.at[e, n]))
    return copies


def slot_of(meta, j):
    return 2 * lax.rem(meta[3] + j % 4 + 4 - meta[2], 4) + j // 4


def transposed_product(meta, r, atts, write):
    r_t = r.T
    for j in range(8):
        val = jnp.dot(r_t, atts[j % 4, j // 4], preferred_element_type=F32)
        for k in range(4):
            write(lax.rem(k + 4 - meta[0], 4), slot_of(meta, j), val[96 * k:96 * (k + 1)])


def residual_kernel(meta, *refs):
    atts, parts = refs[:5], refs[5:7]
    target, res_ref, prod_ref, abuf, attbuf, sem, att_sem = refs[7:]
    slots = [attbuf.at[0], attbuf.at[1], attbuf.at[3], attbuf.at[2, 0], attbuf.at[2, 1]]
    off = pl.multiple_of(meta[4] * TILE, TILE)
    align_loads, att_loads = {}, {}
    for e, loads in ((0, (0,)), (1, (1,)), (3, (2,)), (2, (3, 4))):
        align_loads[e] = fetch_all(part_copies(meta, parts, abuf, sem, pl.ds(off, TILE), e))
        att_loads[e] = fetch_all([pltpu.make_async_copy(atts[n], slots[n], att_sem.at[n]) for n in loads])
    acc = -target[:, pl.ds(off, TILE)].astype(F32)
    for e in (0, 1, 3, 2):
        wait_all(align_loads[e])
        wait_all(att_loads[e])
        for z in range(2):
            acc = acc + jnp.dot(attbuf[e, z], abuf[e, z], preferred_element_type=F32)
    residual = acc.astype(BF16)
    res_ref[...] = residual

    def write(d, g, val):
        prod_ref[d, g] = val.astype(BF16)

    transposed_product(meta, residual, attbuf, write)


def attn_grad_kernel(meta, *refs):
    res_here, res_away, parts = refs[0], refs[1], refs[2:4]
    here, right, left, far_right, far_left = refs[5:10]
    abuf, sem = refs[10:]
    outs = [here.at[0], right.at[0], far_right, left.at[0], here.at[1], right.at[1], far_left, left.at[1]]
    order = (2, 1, 3, 0)
    loads = {e: fetch_all(part_copies(meta, parts, abuf, sem, pl.ds(0, 2 * TILE), e)) for e in order}
    first = meta[1] == 0
    low = jnp.where(first, res_here[...], res_away[...])
    high = jnp.where(first, res_away[...], res_here[...])
    contract = (((1,), (1,)), ((), ()))
    for e in order:
        wait_all(loads[e])
        for z in range(2):
            val = lax.dot_general(low, abuf[e, z, :, :TILE], contract, preferred_element_type=F32)
            val = val + lax.dot_general(high, abuf[e, z, :, TILE:], contract, preferred_element_type=F32)
            outs[4 * z + e][...] = val.astype(BF16)


def pair_kernel(own, arrived, here, right, left, far_right, far_left):
    def pair(d):
        return (own[d].astype(F32) + arrived[d].astype(F32)).astype(BF16)

    far = pair(2)
    far_right[...] = far[:4]
    far_left[...] = far[4:]
    right[...] = pair(1)
    left[...] = pair(3)
    here[...] = pair(0)


def add_far_kernel(right, left, from_left, from_right, right_out, left_out):
    half = right.shape[0] // 2
    right_out[half:] = right[half:]
    right_out[:half] = (right[:half].astype(F32) + from_left[...].astype(F32)).astype(BF16)
    left_out[:half] = left[:half]
    left_out[half:] = (left[half:].astype(F32) + from_right[...].astype(F32)).astype(BF16)


SMEM = pl.BlockSpec(memory_space=pltpu.SMEM)
VMEM = pl.BlockSpec(memory_space=pltpu.VMEM)
ANY = pl.BlockSpec(memory_space=pl.ANY)


def residual_half(meta, half, atts, parts, target, name):
    return pl.pallas_call(
        residual_kernel,
        in_specs=[SMEM] + [ANY] * 7 + [VMEM],
        out_specs=[VMEM] * 2,
        out_shape=[jax.ShapeDtypeStruct((TILE, TILE), BF16), jax.ShapeDtypeStruct((4, 8, 96, TILE), BF16)],
        scratch_shapes=[
            pltpu.VMEM((4, 2, TILE, TILE), BF16),
            pltpu.VMEM((4, 2, TILE, TILE), BF16),
            pltpu.SemaphoreType.DMA((4, 2)),
            pltpu.SemaphoreType.DMA((5,)),
        ],
        compiler_params=PARAMS,
        cost_estimate=SMALL,
        name=name,
    )(jnp.concatenate([meta, half.reshape(1)]).astype(jnp.int32), *atts, *parts, target)


def gradients(meta, atts, parts, target):
    c = meta[1]
    away, product = residual_half(meta, 1 - c, atts, parts, target, "residual_away")
    arrived = shift(product, "c", 1)
    target = after(target, away)
    here, product = residual_half(meta, c, atts, parts, target, "residual_here")
    half_piece = jax.ShapeDtypeStruct((4, 96, TILE), BF16)
    whole_piece = jax.ShapeDtypeStruct((8, 96, TILE), BF16)
    keep, right, left, far_right, far_left = pl.pallas_call(
        pair_kernel,
        in_specs=[VMEM] * 2,
        out_specs=[VMEM] * 5,
        out_shape=[whole_piece] * 3 + [half_piece] * 2,
        compiler_params=PARAMS,
        cost_estimate=SMALL,
        name="core_pair_sum",
    )(product, arrived)
    partials = pl.pallas_call(
        attn_grad_kernel,
        in_specs=[SMEM, VMEM, VMEM] + [ANY] * 3,
        out_specs=[VMEM] * 5,
        out_shape=[jax.ShapeDtypeStruct((2, TILE, TILE), BF16)] * 3 + [jax.ShapeDtypeStruct((TILE, TILE), BF16)] * 2,
        scratch_shapes=[pltpu.VMEM((4, 2, TILE, 2 * TILE), BF16), pltpu.SemaphoreType.DMA((4, 2))],
        compiler_params=PARAMS,
        cost_estimate=SMALL,
        name="attn_grad_terms",
    )(meta, here, away, *parts, far_right)
    grad_terms = (keep, right, left, far_right, far_left)
    return partials, grad_terms


def ring_far(terms, axis, earlier):
    far_right, far_left = terms[3:]
    return after(shift(far_right, axis, 1), earlier), shift(far_left, axis, -1)


def ring_near(terms, arrived, axis, name):
    keep, right, left = terms[:3]
    arrived = [a.reshape((-1,) + right.shape[1:]) for a in arrived]
    right, left = pl.pallas_call(
        add_far_kernel,
        in_specs=[VMEM] * 4,
        out_specs=[VMEM] * 2,
        out_shape=[jax.ShapeDtypeStruct(right.shape, BF16)] * 2,
        compiler_params=PARAMS,
        cost_estimate=SMALL,
        name=name,
    )(right, left, *arrived)
    return shift(right, axis, 1), shift(left, axis, -1)


def sum_terms(*terms):
    total = terms[0].astype(F32)
    for term in terms[1:]:
        total = total + term.astype(F32)
    return total.astype(BF16)


def ring_gather(own, axis, *earlier):
    ahead, behind = shift(own, axis, -1), shift(own, axis, 1)
    half = own.shape[0] // 2
    far_low = shift(after(behind, *earlier)[:half], axis, 1)
    far_high = shift(after(ahead, *earlier)[half:], axis, -1)
    return ahead, behind, far_low, far_high


def block_of(x):
    return 2 * (x % 2) + x // 2


def copy_all_kernel(meta, plan, *refs):
    count = len(refs) - 1
    sem = refs[count]
    loads = [pltpu.make_async_copy(src, dst, sem.at[n]) for n, (src, dst) in enumerate(plan(meta, refs[:count]))]
    wait_all(fetch_all(loads))


def copy_all(meta, plan, copies, arrays, outs, name):
    return pl.pallas_call(
        lambda meta_ref, *refs: copy_all_kernel(meta_ref, plan, *refs),
        in_specs=[SMEM] + [ANY] * len(arrays),
        out_specs=[VMEM] * len(outs),
        out_shape=[jax.ShapeDtypeStruct(shape, BF16) for shape in outs],
        scratch_shapes=[pltpu.SemaphoreType.DMA((copies,))],
        compiler_params=pltpu.CompilerParams(vmem_limit_bytes=60 * 2**20),
        cost_estimate=SMALL,
        name=name,
    )(meta, *arrays)


def first_copies(meta, key_rows, value_rows, alignment, panels):
    tokens, width = key_rows.shape
    model = alignment.shape[1]
    block = panels.shape[1] // 2

    def plan(meta, refs):
        k, v, a, p, both, rows, give = refs
        return [
            (a.at[pl.ds(pl.multiple_of(meta[0] * 48, 48), 48)], rows),
            (k, both.at[:, pl.ds(0, width)]),
            (v, both.at[:, pl.ds(width, width)]),
            (p.at[pl.ds(pl.multiple_of(meta[1] * TILE, TILE), TILE),
                  pl.ds(pl.multiple_of(meta[2] * block, block), block)], give),
        ]

    outs = [(tokens, 2 * width), (48, model), (TILE, block)]
    return copy_all(meta, plan, 4, (key_rows, value_rows, alignment, panels), outs, "first_copies")


def alignment_own(rows, got_rows, x):
    width = rows.shape[1] // 4
    blocks = jnp.stack([block_of(lax.rem(x + 4 - e, 4)) for e in range(4)]).astype(jnp.int32)

    def plan(meta, refs):
        own, got = refs[:2]
        pairs = []
        for e in range(4):
            cols = pl.ds(pl.multiple_of(meta[e] * width, width), width)
            pairs += [(own.at[:, cols], refs[2 + e].at[0]), (got.at[:, cols], refs[2 + e].at[1])]
        return pairs

    pieces = copy_all(blocks, plan, 8, (rows, got_rows), [(2, 48, width)] * 4, "alignment_cut")
    return jnp.stack([shift(pieces[e], "x", -e) if e else pieces[0] for e in range(4)])


def alignment_parts(own, y, att_got, *earlier):
    width = own.shape[3]
    ahead, behind, far_low, far_high = ring_gather(own, "y", att_got)

    def assemble(meta, refs):
        def rows(d):
            return pl.ds(pl.multiple_of(lax.rem(meta[0] + d, 4) * 48, 48), 48)

        out = refs[5]
        return [
            (refs[0], out.at[:, :, rows(0), :]),
            (refs[1], out.at[:, :, rows(1), :]),
            (refs[2], out.at[:, :, rows(3), :]),
            (refs[3], out.at[pl.ds(0, 2), :, rows(2), :]),
            (refs[4], out.at[pl.ds(2, 2), :, rows(2), :]),
        ]

    arrays = (after(own, *earlier), ahead, behind, far_low, far_high)
    mine = copy_all(y.reshape(1), assemble, 5, arrays, [(4, 2, 192, width)], "alignment_rows")[0]
    return mine, shift(mine, "c", 1)


def own_pick(panels, tap_pick, got, tile, p):
    width = panels.shape[1] // 2
    rows = lax.dynamic_slice(panels, (tile * TILE, p * width), (TILE, width))
    tap = lax.dynamic_index_in_dim(tap_pick, tile, 0, keepdims=False)
    return jnp.where((tap & 1) == p, rows, got)


def on_device(queries, key_rows, value_rows, neighbours, tile_counts, panels, alignment, tap_pick):
    zh, x, zl, y, c = (lax.axis_index(name) for name in ("zh", "x", "zl", "y", "c"))
    seq = (zl * 4 + y) * 2 + c
    count = 32
    up = [(i, i + 1) for i in range(count - 1)]
    down = [(i + 1, i) for i in range(count - 1)]
    p = x // 2
    start = jnp.stack([4 * c + y, 1 - zh, 1 - p]).astype(jnp.int32)
    both, rows, give = first_copies(start, key_rows, value_rows, alignment, panels)
    halo = (lax.ppermute(both, SEQ, up), both, lax.ppermute(both, SEQ, down))
    local_ids = neighbours - (seq - 1) * 2

    def attend(tile):
        meta = jnp.concatenate([
            tile.reshape(1),
            lax.dynamic_slice_in_dim(tile_counts, tile, 1),
            lax.dynamic_slice_in_dim(local_ids, tile, 1, 0).reshape(NB),
        ]).astype(jnp.int32)
        return tile_attention(meta, queries, halo)

    got_rows = shift(rows, "zh", 1)
    got = shift(give, "x", 2)
    pick_away = own_pick(panels, tap_pick, got, 1 - zh, p)
    att_send = attend(1 - zh)
    att_got = shift(att_send, "zh", 1)
    later_p = after(p, got, got_rows, att_send)
    width = panels.shape[1] // 2
    give = lax.dynamic_slice(panels, (zh * TILE, (1 - later_p) * width), (TILE, width))
    att_keep = attend(zh)
    own = after(alignment_own(rows, after(got_rows, att_send, pick_away), x), att_keep)
    pick_here = own_pick(panels, tap_pick, after(shift(give, "x", 2), own), zh, p)
    arrived = shift(after(pick_away, att_got, own), "zh", 1)
    att = after(jnp.stack([att_keep, att_got]), own, pick_here)
    ahead, behind, far_low, far_high = ring_gather(att, "x", arrived)
    atts = (att, ahead, behind, far_low.reshape(TILE, TILE), far_high.reshape(TILE, TILE))
    parts = alignment_parts(own, y, att_got, ahead, behind, arrived)
    tap = lax.dynamic_index_in_dim(tap_pick, zh, 0, keepdims=False)
    target = jnp.where(tap // 2 == zh, after(pick_here, ahead, behind), arrived)
    meta = jnp.stack([y, c, zl, x]).astype(jnp.int32)
    attn_terms, align_terms = gradients(meta, atts, parts, target)
    align_near = ring_near(align_terms, ring_far(align_terms, "y", attn_terms[0]), "y", "align_add_far")
    attn_near = ring_near(attn_terms, ring_far(attn_terms, "x", attn_terms[0]), "x", "attn_add_far")
    total = sum_terms(align_terms[0], *align_near).reshape(4, 2, 96, TILE)
    spread = sum_terms(total[0], *[shift(total[d], "zl", d) for d in (1, 2, 3)])
    attn_sum = sum_terms(attn_terms[0], *attn_near)
    attn_here = attn_sum[0]
    attn_away = shift(attn_sum[1], "zh", 1)
    grad_attn = jnp.concatenate([
        jnp.where(zh == 0, attn_here, attn_away),
        jnp.where(zh == 0, attn_away, attn_here),
    ])

    block = sum_terms(spread[0], shift(spread[1], "zh", 1))
    sizes = (2, 4, 4, 4, 2)
    moves = []
    for index in range(256):
        h, i, l, j, k = (int(n) for n in np.unravel_index(index, sizes))
        dest = (h, l, block_of(i), 2 * k + j // 2, j % 2)
        moves.append((index, int(np.ravel_multi_index(dest, sizes))))
    grad_align = lax.ppermute(block, SEG + SEQ, moves).T.astype(F32)
    return grad_align, grad_attn


def solution(mesh):
    fine = Mesh(mesh.devices.reshape(2, 4, 4, 4, 2), SEG + SEQ)
    placed = (
        P(SEQ, SEG),
        P(SEQ, SEG),
        P(SEQ, SEG),
        P(SEQ, None),
        P(SEQ),
        P(SEQ, SEG),
        P(SEG, None),
        P(SEQ),
    )
    return jax.shard_map(
        on_device,
        mesh=fine,
        in_specs=placed,
        out_specs=(P(SEG, SEQ), P(SEQ, SEG)),
        check_vma=False,
    )
```

```python
import jax
import jax.numpy as jnp
import numpy as np
from jax import lax
from jax.experimental import pallas as pl
from jax.experimental.pallas import tpu as pltpu
from jax.sharding import Mesh, PartitionSpec as P

HDIM = 128
TILE = 384
NB = 4
LOG2E = 1.4426950408889634
F32 = jnp.float32
BF16 = jnp.bfloat16
SEQ = ("zl", "y", "c")
SEG = ("zh", "x")
SMALL = pl.CostEstimate(flops=1, bytes_accessed=1, transcendentals=0)
PARAMS = pltpu.CompilerParams(vmem_limit_bytes=24 * 2**20)


def shift(a, axis, d):
    n = lax.axis_size(axis)
    return lax.ppermute(a, axis, [(i, (i + d) % n) for i in range(n)])


def after(value, *earlier):
    return lax.optimization_barrier((value, *earlier))[0]


def attn_kernel(meta, q_ref, before, here, after, out_ref, kvbuf, scores, sem):
    width = q_ref.shape[1]
    heads = width // HDIM
    count = meta[1]
    for half in range(2):
        cols = pl.ds(half * width, width)
        for j in range(NB):
            tile = meta[2 + j]
            for part, ref in enumerate((before, here, after)):
                @pl.when(tile // 2 == part)
                def _():
                    rows = pl.ds(pl.multiple_of((tile - 2 * part) * TILE, TILE), TILE)
                    pltpu.make_async_copy(ref.at[rows, cols], kvbuf.at[half, j], sem.at[half, j]).start()

    def arrive(half):
        for j in range(NB):
            cols = pl.ds(half * width, width)
            pltpu.make_async_copy(here.at[pl.ds(0, TILE), cols], kvbuf.at[half, j], sem.at[half, j]).wait()

    arrive(0)
    arrive(1)
    factor = HDIM ** (-0.5) * LOG2E
    for h in range(heads):
        cols = slice(h * HDIM, (h + 1) * HDIM)
        q = q_ref[:, cols]
        top = None
        for j in range(NB):
            s = lax.dot_general(q, kvbuf[0, j, :, cols], (((1,), (1,)), ((), ())), preferred_element_type=F32)
            if j >= 2:
                s = jnp.where(j < count, s, -jnp.inf)
            scores[:, j * TILE:(j + 1) * TILE] = s
            m = jnp.max(s, axis=1, keepdims=True)
            top = m if top is None else jnp.maximum(top, m)
        total = None
        acc = None
        for j in range(NB):
            e = jnp.exp2((scores[:, j * TILE:(j + 1) * TILE] - top) * factor)
            part = jnp.sum(e, axis=1, keepdims=True)
            total = part if total is None else total + part
            o = jnp.dot(e.astype(BF16), kvbuf[1, j, :, cols], preferred_element_type=F32)
            acc = o if acc is None else acc + o
        out_ref[:, cols] = (acc / total).astype(BF16)


def tile_attention(meta, queries, halo):
    width = queries.shape[1]
    grid_spec = pltpu.PrefetchScalarGridSpec(
        num_scalar_prefetch=1,
        grid=(1,),
        in_specs=[pl.BlockSpec((TILE, width), lambda i, meta: (meta[0], 0))]
        + [pl.BlockSpec(memory_space=pl.ANY)] * 3,
        out_specs=pl.BlockSpec((TILE, width), lambda i, meta: (0, 0)),
        scratch_shapes=[
            pltpu.VMEM((2, NB, TILE, width), BF16),
            pltpu.VMEM((TILE, NB * TILE), F32),
            pltpu.SemaphoreType.DMA((2, NB)),
        ],
    )
    return pl.pallas_call(
        attn_kernel,
        grid_spec=grid_spec,
        out_shape=jax.ShapeDtypeStruct((TILE, width), BF16),
        compiler_params=PARAMS,
        cost_estimate=SMALL,
        name="tile_attention",
    )(meta, queries, *halo)


def fetch_all(copies):
    for copy in copies:
        copy.start()
    return copies


def wait_all(copies):
    for copy in copies:
        copy.wait()


def part_copies(meta, parts, abuf, sem, cols, e):
    copies = []
    for n, ref in enumerate(parts):
        step = ref.shape[2]
        rows = pl.ds(pl.multiple_of(jnp.bitwise_xor(meta[1], n) * step, step), step)
        copies.append(pltpu.make_async_copy(ref.at[e, :, :, cols], abuf.at[e, :, rows, :], sem.at[e, n]))
    return copies


def slot_of(meta, j):
    return 2 * lax.rem(meta[3] + j % 4 + 4 - meta[2], 4) + j // 4


def transposed_product(meta, r, atts, write):
    r_t = r.T
    for j in range(8):
        val = jnp.dot(r_t, atts[j % 4, j // 4], preferred_element_type=F32)
        for k in range(4):
            write(lax.rem(k + 4 - meta[0], 4), slot_of(meta, j), val[96 * k:96 * (k + 1)])


def residual_kernel(meta, *refs):
    atts, parts = refs[:5], refs[5:7]
    target, res_ref, prod_ref, abuf, attbuf, sem, att_sem = refs[7:]
    slots = [attbuf.at[0], attbuf.at[1], attbuf.at[3], attbuf.at[2, 0], attbuf.at[2, 1]]
    off = pl.multiple_of(meta[4] * TILE, TILE)
    align_loads, att_loads = {}, {}
    for e, loads in ((0, (0,)), (1, (1,)), (3, (2,)), (2, (3, 4))):
        align_loads[e] = fetch_all(part_copies(meta, parts, abuf, sem, pl.ds(off, TILE), e))
        att_loads[e] = fetch_all([pltpu.make_async_copy(atts[n], slots[n], att_sem.at[n]) for n in loads])
    acc = -target[:, pl.ds(off, TILE)].astype(F32)
    for e in (0, 1, 3, 2):
        wait_all(align_loads[e])
        wait_all(att_loads[e])
        for z in range(2):
            acc = acc + jnp.dot(attbuf[e, z], abuf[e, z], preferred_element_type=F32)
    residual = acc.astype(BF16)
    res_ref[...] = residual

    def write(d, g, val):
        prod_ref[d, g] = val.astype(BF16)

    transposed_product(meta, residual, attbuf, write)


def attn_grad_kernel(meta, *refs):
    res_here, res_away, parts = refs[0], refs[1], refs[2:4]
    here, right, left, far_right, far_left = refs[5:10]
    abuf, sem = refs[10:]
    outs = [here.at[0], right.at[0], far_right, left.at[0], here.at[1], right.at[1], far_left, left.at[1]]
    order = (2, 1, 3, 0)
    loads = {e: fetch_all(part_copies(meta, parts, abuf, sem, pl.ds(0, 2 * TILE), e)) for e in order}
    first = meta[1] == 0
    low = jnp.where(first, res_here[...], res_away[...])
    high = jnp.where(first, res_away[...], res_here[...])
    contract = (((1,), (1,)), ((), ()))
    for e in order:
        wait_all(loads[e])
        for z in range(2):
            val = lax.dot_general(low, abuf[e, z, :, :TILE], contract, preferred_element_type=F32)
            val = val + lax.dot_general(high, abuf[e, z, :, TILE:], contract, preferred_element_type=F32)
            outs[4 * z + e][...] = val.astype(BF16)


def pair_kernel(own, arrived, here, right, left, far_right, far_left):
    def pair(d):
        return (own[d].astype(F32) + arrived[d].astype(F32)).astype(BF16)

    far = pair(2)
    far_right[...] = far[:4]
    far_left[...] = far[4:]
    right[...] = pair(1)
    left[...] = pair(3)
    here[...] = pair(0)


def add_far_kernel(right, left, from_left, from_right, right_out, left_out):
    half = right.shape[0] // 2
    right_out[half:] = right[half:]
    right_out[:half] = (right[:half].astype(F32) + from_left[...].astype(F32)).astype(BF16)
    left_out[:half] = left[:half]
    left_out[half:] = (left[half:].astype(F32) + from_right[...].astype(F32)).astype(BF16)


SMEM = pl.BlockSpec(memory_space=pltpu.SMEM)
VMEM = pl.BlockSpec(memory_space=pltpu.VMEM)
ANY = pl.BlockSpec(memory_space=pl.ANY)


def residual_half(meta, half, atts, parts, target, name):
    return pl.pallas_call(
        residual_kernel,
        in_specs=[SMEM] + [ANY] * 7 + [VMEM],
        out_specs=[VMEM] * 2,
        out_shape=[jax.ShapeDtypeStruct((TILE, TILE), BF16), jax.ShapeDtypeStruct((4, 8, 96, TILE), BF16)],
        scratch_shapes=[
            pltpu.VMEM((4, 2, TILE, TILE), BF16),
            pltpu.VMEM((4, 2, TILE, TILE), BF16),
            pltpu.SemaphoreType.DMA((4, 2)),
            pltpu.SemaphoreType.DMA((5,)),
        ],
        compiler_params=PARAMS,
        cost_estimate=SMALL,
        name=name,
    )(jnp.concatenate([meta, half.reshape(1)]).astype(jnp.int32), *atts, *parts, target)


def gradients(meta, atts, parts, target):
    c = meta[1]
    away, product = residual_half(meta, 1 - c, atts, parts, target, "residual_away")
    arrived = shift(product, "c", 1)
    target = after(target, away)
    here, product = residual_half(meta, c, atts, parts, target, "residual_here")
    half_piece = jax.ShapeDtypeStruct((4, 96, TILE), BF16)
    whole_piece = jax.ShapeDtypeStruct((8, 96, TILE), BF16)
    keep, right, left, far_right, far_left = pl.pallas_call(
        pair_kernel,
        in_specs=[VMEM] * 2,
        out_specs=[VMEM] * 5,
        out_shape=[whole_piece] * 3 + [half_piece] * 2,
        compiler_params=PARAMS,
        cost_estimate=SMALL,
        name="core_pair_sum",
    )(product, arrived)
    partials = pl.pallas_call(
        attn_grad_kernel,
        in_specs=[SMEM, VMEM, VMEM] + [ANY] * 3,
        out_specs=[VMEM] * 5,
        out_shape=[jax.ShapeDtypeStruct((2, TILE, TILE), BF16)] * 3 + [jax.ShapeDtypeStruct((TILE, TILE), BF16)] * 2,
        scratch_shapes=[pltpu.VMEM((4, 2, TILE, 2 * TILE), BF16), pltpu.SemaphoreType.DMA((4, 2))],
        compiler_params=PARAMS,
        cost_estimate=SMALL,
        name="attn_grad_terms",
    )(meta, here, away, *parts, far_right)
    grad_terms = (keep, right, left, far_right, far_left)
    return partials, grad_terms


def ring_far(terms, axis, earlier):
    far_right, far_left = terms[3:]
    return after(shift(far_right, axis, 1), earlier), shift(far_left, axis, -1)


def ring_near(terms, arrived, axis, name):
    keep, right, left = terms[:3]
    arrived = [a.reshape((-1,) + right.shape[1:]) for a in arrived]
    right, left = pl.pallas_call(
        add_far_kernel,
        in_specs=[VMEM] * 4,
        out_specs=[VMEM] * 2,
        out_shape=[jax.ShapeDtypeStruct(right.shape, BF16)] * 2,
        compiler_params=PARAMS,
        cost_estimate=SMALL,
        name=name,
    )(right, left, *arrived)
    return shift(right, axis, 1), shift(left, axis, -1)


def sum_terms(*terms):
    total = terms[0].astype(F32)
    for term in terms[1:]:
        total = total + term.astype(F32)
    return total.astype(BF16)


def ring_gather(own, axis):
    ahead, behind = shift(own, axis, -1), shift(own, axis, 1)
    half = own.shape[0] // 2
    far_low = shift(behind[:half], axis, 1)
    far_high = shift(ahead[half:], axis, -1)
    return ahead, behind, far_low, far_high


def block_of(x):
    return 2 * (x % 2) + x // 2


def copy_all_kernel(meta, plan, *refs):
    count = len(refs) - 1
    sem = refs[count]
    loads = [pltpu.make_async_copy(src, dst, sem.at[n]) for n, (src, dst) in enumerate(plan(meta, refs[:count]))]
    wait_all(fetch_all(loads))


def copy_all(meta, plan, copies, arrays, outs, name):
    return pl.pallas_call(
        lambda meta_ref, *refs: copy_all_kernel(meta_ref, plan, *refs),
        in_specs=[SMEM] + [ANY] * len(arrays),
        out_specs=[VMEM] * len(outs),
        out_shape=[jax.ShapeDtypeStruct(shape, BF16) for shape in outs],
        scratch_shapes=[pltpu.SemaphoreType.DMA((copies,))],
        compiler_params=pltpu.CompilerParams(vmem_limit_bytes=60 * 2**20),
        cost_estimate=SMALL,
        name=name,
    )(meta, *arrays)


def first_copies(meta, key_rows, value_rows, alignment, panels):
    tokens, width = key_rows.shape
    model = alignment.shape[1]
    block = panels.shape[1] // 2

    def plan(meta, refs):
        k, v, a, p, both, rows, give = refs
        return [
            (a.at[pl.ds(pl.multiple_of(meta[0] * 48, 48), 48)], rows),
            (k, both.at[:, pl.ds(0, width)]),
            (v, both.at[:, pl.ds(width, width)]),
            (p.at[pl.ds(pl.multiple_of(meta[1] * TILE, TILE), TILE),
                  pl.ds(pl.multiple_of(meta[2] * block, block), block)], give),
        ]

    outs = [(tokens, 2 * width), (48, model), (TILE, block)]
    return copy_all(meta, plan, 4, (key_rows, value_rows, alignment, panels), outs, "first_copies")


def alignment_own(rows, got_rows, x):
    width = rows.shape[1] // 4
    blocks = jnp.stack([block_of(lax.rem(x + 4 - e, 4)) for e in range(4)]).astype(jnp.int32)

    def plan(meta, refs):
        own, got = refs[:2]
        pairs = []
        for e in range(4):
            cols = pl.ds(pl.multiple_of(meta[e] * width, width), width)
            pairs += [(own.at[:, cols], refs[2 + e].at[0]), (got.at[:, cols], refs[2 + e].at[1])]
        return pairs

    pieces = copy_all(blocks, plan, 8, (rows, got_rows), [(2, 48, width)] * 4, "alignment_cut")
    return jnp.stack([shift(pieces[e], "x", -e) if e else pieces[0] for e in range(4)])


def alignment_parts(own, y, arrived, *earlier):
    width = own.shape[3]
    ahead, behind, far_low, far_high = ring_gather(own, "y")

    def assemble(meta, refs):
        def rows(d):
            return pl.ds(pl.multiple_of(lax.rem(meta[0] + d, 4) * 48, 48), 48)

        out = refs[5]
        return [
            (refs[0], out.at[:, :, rows(0), :]),
            (refs[1], out.at[:, :, rows(1), :]),
            (refs[2], out.at[:, :, rows(3), :]),
            (refs[3], out.at[pl.ds(0, 2), :, rows(2), :]),
            (refs[4], out.at[pl.ds(2, 2), :, rows(2), :]),
        ]

    arrays = (after(own, *earlier), ahead, behind, far_low, far_high)
    mine = copy_all(y.reshape(1), assemble, 5, arrays, [(4, 2, 192, width)], "alignment_rows")[0]
    return mine, shift(after(mine, arrived), "c", 1)


def own_pick(panels, tap_pick, got, tile, p):
    width = panels.shape[1] // 2
    rows = lax.dynamic_slice(panels, (tile * TILE, p * width), (TILE, width))
    tap = lax.dynamic_index_in_dim(tap_pick, tile, 0, keepdims=False)
    return jnp.where((tap & 1) == p, rows, got)


def on_device(queries, key_rows, value_rows, neighbours, tile_counts, panels, alignment, tap_pick):
    zh, x, zl, y, c = (lax.axis_index(name) for name in ("zh", "x", "zl", "y", "c"))
    seq = (zl * 4 + y) * 2 + c
    count = 32
    up = [(i, i + 1) for i in range(count - 1)]
    down = [(i + 1, i) for i in range(count - 1)]
    p = x // 2
    start = jnp.stack([4 * c + y, 1 - zh, 1 - p]).astype(jnp.int32)
    both, rows, give = first_copies(start, key_rows, value_rows, alignment, panels)
    halo = (lax.ppermute(both, SEQ, up), both, lax.ppermute(both, SEQ, down))
    local_ids = neighbours - (seq - 1) * 2

    def attend(tile):
        meta = jnp.concatenate([
            tile.reshape(1),
            lax.dynamic_slice_in_dim(tile_counts, tile, 1),
            lax.dynamic_slice_in_dim(local_ids, tile, 1, 0).reshape(NB),
        ]).astype(jnp.int32)
        return tile_attention(meta, queries, halo)

    got_rows = shift(rows, "zh", 1)
    got = shift(give, "x", 2)
    pick_away = own_pick(panels, tap_pick, got, 1 - zh, p)
    att_send = attend(1 - zh)
    att_got = shift(att_send, "zh", 1)
    later_p = after(p, got, got_rows, att_send)
    width = panels.shape[1] // 2
    give = lax.dynamic_slice(panels, (zh * TILE, (1 - later_p) * width), (TILE, width))
    att_keep = attend(zh)
    own = after(alignment_own(rows, after(got_rows, att_send), x), att_keep, att_got)
    pick_here = own_pick(panels, tap_pick, after(shift(give, "x", 2), own), zh, p)
    arrived = shift(after(pick_away, att_got, own), "zh", 1)
    att = after(jnp.stack([att_keep, att_got]), own, pick_here)
    ahead, behind, far_low, far_high = ring_gather(att, "x")
    atts = (att, ahead, behind, far_low.reshape(TILE, TILE), far_high.reshape(TILE, TILE))
    parts = alignment_parts(own, y, arrived, far_low, far_high)
    tap = lax.dynamic_index_in_dim(tap_pick, zh, 0, keepdims=False)
    target = jnp.where(tap // 2 == zh, after(pick_here, ahead, behind), arrived)
    meta = jnp.stack([y, c, zl, x]).astype(jnp.int32)
    attn_terms, align_terms = gradients(meta, atts, parts, target)
    align_near = ring_near(align_terms, ring_far(align_terms, "y", attn_terms[0]), "y", "align_add_far")
    attn_near = ring_near(attn_terms, ring_far(attn_terms, "x", attn_terms[0]), "x", "attn_add_far")
    total = sum_terms(align_terms[0], *align_near).reshape(4, 2, 96, TILE)
    spread = sum_terms(total[0], *[shift(total[d], "zl", d) for d in (1, 2, 3)])
    attn_sum = sum_terms(attn_terms[0], *attn_near)
    attn_here = attn_sum[0]
    attn_away = shift(attn_sum[1], "zh", 1)
    grad_attn = jnp.concatenate([
        jnp.where(zh == 0, attn_here, attn_away),
        jnp.where(zh == 0, attn_away, attn_here),
    ])

    block = sum_terms(spread[0], shift(spread[1], "zh", 1))
    sizes = (2, 4, 4, 4, 2)
    moves = []
    for index in range(256):
        h, i, l, j, k = (int(n) for n in np.unravel_index(index, sizes))
        dest = (h, l, block_of(i), 2 * k + j // 2, j % 2)
        moves.append((index, int(np.ravel_multi_index(dest, sizes))))
    grad_align = lax.ppermute(block, SEG + SEQ, moves).T.astype(F32)
    return grad_align, grad_attn


def solution(mesh):
    fine = Mesh(mesh.devices.reshape(2, 4, 4, 4, 2), SEG + SEQ)
    placed = (
        P(SEQ, SEG),
        P(SEQ, SEG),
        P(SEQ, SEG),
        P(SEQ, None),
        P(SEQ),
        P(SEQ, SEG),
        P(SEG, None),
        P(SEQ),
    )
    return jax.shard_map(
        on_device,
        mesh=fine,
        in_specs=placed,
        out_specs=(P(SEG, SEQ), P(SEQ, SEG)),
        check_vma=False,
    )
```

```python
import jax
import jax.numpy as jnp
import numpy as np
from jax import lax
from jax.experimental import pallas as pl
from jax.experimental.pallas import tpu as pltpu
from jax.sharding import Mesh, PartitionSpec as P

HDIM = 128
TILE = 384
NB = 4
LOG2E = 1.4426950408889634
F32 = jnp.float32
BF16 = jnp.bfloat16
SEQ = ("zl", "y", "c")
SEG = ("zh", "x")
SMALL = pl.CostEstimate(flops=1, bytes_accessed=1, transcendentals=0)
PARAMS = pltpu.CompilerParams(vmem_limit_bytes=24 * 2**20)


def shift(a, axis, d):
    n = lax.axis_size(axis)
    return lax.ppermute(a, axis, [(i, (i + d) % n) for i in range(n)])


def after(value, *earlier):
    return lax.optimization_barrier((value, *earlier))[0]


def attn_kernel(meta, q_ref, before, here, after, out_ref, kvbuf, scores, sem):
    width = q_ref.shape[1]
    heads = width // HDIM
    count = meta[1]
    for half in range(2):
        cols = pl.ds(half * width, width)
        for j in range(NB):
            tile = meta[2 + j]
            for part, ref in enumerate((before, here, after)):
                @pl.when(tile // 2 == part)
                def _():
                    rows = pl.ds(pl.multiple_of((tile - 2 * part) * TILE, TILE), TILE)
                    pltpu.make_async_copy(ref.at[rows, cols], kvbuf.at[half, j], sem.at[half, j]).start()

    def arrive(half):
        for j in range(NB):
            cols = pl.ds(half * width, width)
            pltpu.make_async_copy(here.at[pl.ds(0, TILE), cols], kvbuf.at[half, j], sem.at[half, j]).wait()

    arrive(0)
    arrive(1)
    factor = HDIM ** (-0.5) * LOG2E
    for h in range(heads):
        cols = slice(h * HDIM, (h + 1) * HDIM)
        q = q_ref[:, cols]
        top = None
        for j in range(NB):
            s = lax.dot_general(q, kvbuf[0, j, :, cols], (((1,), (1,)), ((), ())), preferred_element_type=F32)
            if j >= 2:
                s = jnp.where(j < count, s, -jnp.inf)
            scores[:, j * TILE:(j + 1) * TILE] = s
            m = jnp.max(s, axis=1, keepdims=True)
            top = m if top is None else jnp.maximum(top, m)
        total = None
        acc = None
        for j in range(NB):
            e = jnp.exp2((scores[:, j * TILE:(j + 1) * TILE] - top) * factor)
            part = jnp.sum(e, axis=1, keepdims=True)
            total = part if total is None else total + part
            o = jnp.dot(e.astype(BF16), kvbuf[1, j, :, cols], preferred_element_type=F32)
            acc = o if acc is None else acc + o
        out_ref[:, cols] = (acc / total).astype(BF16)


def tile_attention(meta, queries, halo):
    width = queries.shape[1]
    grid_spec = pltpu.PrefetchScalarGridSpec(
        num_scalar_prefetch=1,
        grid=(1,),
        in_specs=[pl.BlockSpec((TILE, width), lambda i, meta: (meta[0], 0))]
        + [pl.BlockSpec(memory_space=pl.ANY)] * 3,
        out_specs=pl.BlockSpec((TILE, width), lambda i, meta: (0, 0)),
        scratch_shapes=[
            pltpu.VMEM((2, NB, TILE, width), BF16),
            pltpu.VMEM((TILE, NB * TILE), F32),
            pltpu.SemaphoreType.DMA((2, NB)),
        ],
    )
    return pl.pallas_call(
        attn_kernel,
        grid_spec=grid_spec,
        out_shape=jax.ShapeDtypeStruct((TILE, width), BF16),
        compiler_params=PARAMS,
        cost_estimate=SMALL,
        name="tile_attention",
    )(meta, queries, *halo)


def fetch_all(copies):
    for copy in copies:
        copy.start()
    return copies


def wait_all(copies):
    for copy in copies:
        copy.wait()


def part_copies(meta, parts, abuf, sem, cols, e):
    copies = []
    for n, ref in enumerate(parts):
        step = ref.shape[2]
        rows = pl.ds(pl.multiple_of(jnp.bitwise_xor(meta[1], n) * step, step), step)
        copies.append(pltpu.make_async_copy(ref.at[e, :, :, cols], abuf.at[e, :, rows, :], sem.at[e, n]))
    return copies


def slot_of(meta, j):
    return 2 * lax.rem(meta[3] + j % 4 + 4 - meta[2], 4) + j // 4


def transposed_product(meta, r, atts, write):
    r_t = r.T
    for j in range(8):
        val = jnp.dot(r_t, atts[j % 4, j // 4], preferred_element_type=F32)
        for k in range(4):
            write(lax.rem(k + 4 - meta[0], 4), slot_of(meta, j), val[96 * k:96 * (k + 1)])


def residual_kernel(meta, *refs):
    atts, parts = refs[:5], refs[5:7]
    target, res_ref, prod_ref, abuf, attbuf, sem, att_sem = refs[7:]
    slots = [attbuf.at[0], attbuf.at[1], attbuf.at[3], attbuf.at[2, 0], attbuf.at[2, 1]]
    off = pl.multiple_of(meta[4] * TILE, TILE)
    align_loads, att_loads = {}, {}
    for e, loads in ((0, (0,)), (1, (1,)), (3, (2,)), (2, (3, 4))):
        align_loads[e] = fetch_all(part_copies(meta, parts, abuf, sem, pl.ds(off, TILE), e))
        att_loads[e] = fetch_all([pltpu.make_async_copy(atts[n], slots[n], att_sem.at[n]) for n in loads])
    acc = -target[:, pl.ds(off, TILE)].astype(F32)
    for e in (0, 1, 3, 2):
        wait_all(align_loads[e])
        wait_all(att_loads[e])
        for z in range(2):
            acc = acc + jnp.dot(attbuf[e, z], abuf[e, z], preferred_element_type=F32)
    residual = acc.astype(BF16)
    res_ref[...] = residual

    def write(d, g, val):
        prod_ref[d, g] = val.astype(BF16)

    transposed_product(meta, residual, attbuf, write)


def attn_grad_kernel(meta, *refs):
    res_here, res_away, parts = refs[0], refs[1], refs[2:4]
    here, right, left, far_right, far_left = refs[5:10]
    abuf, sem = refs[10:]
    outs = [here.at[0], right.at[0], far_right, left.at[0], here.at[1], right.at[1], far_left, left.at[1]]
    order = (2, 1, 3, 0)
    loads = {e: fetch_all(part_copies(meta, parts, abuf, sem, pl.ds(0, 2 * TILE), e)) for e in order}
    first = meta[1] == 0
    low = jnp.where(first, res_here[...], res_away[...])
    high = jnp.where(first, res_away[...], res_here[...])
    contract = (((1,), (1,)), ((), ()))
    for e in order:
        wait_all(loads[e])
        for z in range(2):
            val = lax.dot_general(low, abuf[e, z, :, :TILE], contract, preferred_element_type=F32)
            val = val + lax.dot_general(high, abuf[e, z, :, TILE:], contract, preferred_element_type=F32)
            outs[4 * z + e][...] = val.astype(BF16)


def pair_kernel(own, arrived, here, right, left, far_right, far_left):
    def pair(d):
        return (own[d].astype(F32) + arrived[d].astype(F32)).astype(BF16)

    far = pair(2)
    far_right[...] = far[:4]
    far_left[...] = far[4:]
    right[...] = pair(1)
    left[...] = pair(3)
    here[...] = pair(0)


def add_far_kernel(right, left, from_left, from_right, right_out, left_out):
    half = right.shape[0] // 2
    right_out[half:] = right[half:]
    right_out[:half] = (right[:half].astype(F32) + from_left[...].astype(F32)).astype(BF16)
    left_out[:half] = left[:half]
    left_out[half:] = (left[half:].astype(F32) + from_right[...].astype(F32)).astype(BF16)


SMEM = pl.BlockSpec(memory_space=pltpu.SMEM)
VMEM = pl.BlockSpec(memory_space=pltpu.VMEM)
ANY = pl.BlockSpec(memory_space=pl.ANY)


def residual_half(meta, half, atts, parts, target, name):
    return pl.pallas_call(
        residual_kernel,
        in_specs=[SMEM] + [ANY] * 7 + [VMEM],
        out_specs=[VMEM] * 2,
        out_shape=[jax.ShapeDtypeStruct((TILE, TILE), BF16), jax.ShapeDtypeStruct((4, 8, 96, TILE), BF16)],
        scratch_shapes=[
            pltpu.VMEM((4, 2, TILE, TILE), BF16),
            pltpu.VMEM((4, 2, TILE, TILE), BF16),
            pltpu.SemaphoreType.DMA((4, 2)),
            pltpu.SemaphoreType.DMA((5,)),
        ],
        compiler_params=pltpu.CompilerParams(vmem_limit_bytes=60 * 2**20),
        cost_estimate=SMALL,
        name=name,
    )(jnp.concatenate([meta, half.reshape(1)]).astype(jnp.int32), *atts, *parts, target)


def gradients(meta, atts, parts, target):
    c = meta[1]
    away, product = residual_half(meta, 1 - c, atts, parts, target, "residual_away")
    arrived = shift(product, "c", 1)
    target = after(target, away)
    here, product = residual_half(meta, c, atts, parts, target, "residual_here")
    half_piece = jax.ShapeDtypeStruct((4, 96, TILE), BF16)
    whole_piece = jax.ShapeDtypeStruct((8, 96, TILE), BF16)
    keep, right, left, far_right, far_left = pl.pallas_call(
        pair_kernel,
        in_specs=[VMEM] * 2,
        out_specs=[VMEM] * 5,
        out_shape=[whole_piece] * 3 + [half_piece] * 2,
        compiler_params=PARAMS,
        cost_estimate=SMALL,
        name="core_pair_sum",
    )(product, arrived)
    partials = pl.pallas_call(
        attn_grad_kernel,
        in_specs=[SMEM, VMEM, VMEM] + [ANY] * 3,
        out_specs=[VMEM] * 5,
        out_shape=[jax.ShapeDtypeStruct((2, TILE, TILE), BF16)] * 3 + [jax.ShapeDtypeStruct((TILE, TILE), BF16)] * 2,
        scratch_shapes=[pltpu.VMEM((4, 2, TILE, 2 * TILE), BF16), pltpu.SemaphoreType.DMA((4, 2))],
        compiler_params=PARAMS,
        cost_estimate=SMALL,
        name="attn_grad_terms",
    )(meta, here, away, *parts, far_right)
    grad_terms = (keep, right, left, far_right, far_left)
    return partials, grad_terms


def ring_far(terms, axis, earlier):
    far_right, far_left = terms[3:]
    return after(shift(far_right, axis, 1), earlier), shift(far_left, axis, -1)


def ring_near(terms, arrived, axis, name):
    keep, right, left = terms[:3]
    arrived = [a.reshape((-1,) + right.shape[1:]) for a in arrived]
    right, left = pl.pallas_call(
        add_far_kernel,
        in_specs=[VMEM] * 4,
        out_specs=[VMEM] * 2,
        out_shape=[jax.ShapeDtypeStruct(right.shape, BF16)] * 2,
        compiler_params=PARAMS,
        cost_estimate=SMALL,
        name=name,
    )(right, left, *arrived)
    return shift(right, axis, 1), shift(left, axis, -1)


def sum_terms(*terms):
    total = terms[0].astype(F32)
    for term in terms[1:]:
        total = total + term.astype(F32)
    return total.astype(BF16)


def ring_gather(own, axis):
    ahead, behind = shift(own, axis, -1), shift(own, axis, 1)
    half = own.shape[0] // 2
    far_low = shift(behind[:half], axis, 1)
    far_high = shift(ahead[half:], axis, -1)
    return ahead, behind, far_low, far_high


def block_of(x):
    return 2 * (x % 2) + x // 2


def copy_all_kernel(meta, plan, *refs):
    count = len(refs) - 1
    sem = refs[count]
    loads = [pltpu.make_async_copy(src, dst, sem.at[n]) for n, (src, dst) in enumerate(plan(meta, refs[:count]))]
    wait_all(fetch_all(loads))


def copy_all(meta, plan, copies, arrays, outs, name):
    return pl.pallas_call(
        lambda meta_ref, *refs: copy_all_kernel(meta_ref, plan, *refs),
        in_specs=[SMEM] + [ANY] * len(arrays),
        out_specs=[VMEM] * len(outs),
        out_shape=[jax.ShapeDtypeStruct(shape, BF16) for shape in outs],
        scratch_shapes=[pltpu.SemaphoreType.DMA((copies,))],
        compiler_params=pltpu.CompilerParams(vmem_limit_bytes=60 * 2**20),
        cost_estimate=SMALL,
        name=name,
    )(meta, *arrays)


def first_copies(meta, key_rows, value_rows, alignment, panels):
    tokens, width = key_rows.shape
    model = alignment.shape[1]
    block = panels.shape[1] // 2

    def plan(meta, refs):
        k, v, a, p, both, rows, give = refs
        return [
            (a.at[pl.ds(pl.multiple_of(meta[0] * 48, 48), 48)], rows),
            (k, both.at[:, pl.ds(0, width)]),
            (v, both.at[:, pl.ds(width, width)]),
            (p.at[pl.ds(pl.multiple_of(meta[1] * TILE, TILE), TILE),
                  pl.ds(pl.multiple_of(meta[2] * block, block), block)], give),
        ]

    outs = [(tokens, 2 * width), (48, model), (TILE, block)]
    return copy_all(meta, plan, 4, (key_rows, value_rows, alignment, panels), outs, "first_copies")


def alignment_own(rows, got_rows, x):
    width = rows.shape[1] // 4
    blocks = jnp.stack([block_of(lax.rem(x + 4 - e, 4)) for e in range(4)]).astype(jnp.int32)

    def plan(meta, refs):
        own, got = refs[:2]
        pairs = []
        for e in range(4):
            cols = pl.ds(pl.multiple_of(meta[e] * width, width), width)
            pairs += [(own.at[:, cols], refs[2 + e].at[0]), (got.at[:, cols], refs[2 + e].at[1])]
        return pairs

    pieces = copy_all(blocks, plan, 8, (rows, got_rows), [(2, 48, width)] * 4, "alignment_cut")
    return jnp.stack([shift(pieces[e], "x", -e) if e else pieces[0] for e in range(4)])


def alignment_parts(own, y, arrived, *earlier):
    width = own.shape[3]
    ahead, behind, far_low, far_high = ring_gather(own, "y")

    def assemble(meta, refs):
        def rows(d):
            return pl.ds(pl.multiple_of(lax.rem(meta[0] + d, 4) * 48, 48), 48)

        out = refs[5]
        return [
            (refs[0], out.at[:, :, rows(0), :]),
            (refs[1], out.at[:, :, rows(1), :]),
            (refs[2], out.at[:, :, rows(3), :]),
            (refs[3], out.at[pl.ds(0, 2), :, rows(2), :]),
            (refs[4], out.at[pl.ds(2, 2), :, rows(2), :]),
        ]

    arrays = (after(own, *earlier), ahead, behind, far_low, far_high)
    mine = copy_all(y.reshape(1), assemble, 5, arrays, [(4, 2, 192, width)], "alignment_rows")[0]
    return mine, shift(after(mine, arrived), "c", 1)


def own_pick(panels, tap_pick, got, tile, p):
    width = panels.shape[1] // 2
    rows = lax.dynamic_slice(panels, (tile * TILE, p * width), (TILE, width))
    tap = lax.dynamic_index_in_dim(tap_pick, tile, 0, keepdims=False)
    return jnp.where((tap & 1) == p, rows, got)


def on_device(queries, key_rows, value_rows, neighbours, tile_counts, panels, alignment, tap_pick):
    zh, x, zl, y, c = (lax.axis_index(name) for name in ("zh", "x", "zl", "y", "c"))
    seq = (zl * 4 + y) * 2 + c
    count = 32
    up = [(i, i + 1) for i in range(count - 1)]
    down = [(i + 1, i) for i in range(count - 1)]
    p = x // 2
    start = jnp.stack([4 * c + y, 1 - zh, 1 - p]).astype(jnp.int32)
    both, rows, give = first_copies(start, key_rows, value_rows, alignment, panels)
    halo = (lax.ppermute(both, SEQ, up), both, lax.ppermute(both, SEQ, down))
    local_ids = neighbours - (seq - 1) * 2

    def attend(tile):
        meta = jnp.concatenate([
            tile.reshape(1),
            lax.dynamic_slice_in_dim(tile_counts, tile, 1),
            lax.dynamic_slice_in_dim(local_ids, tile, 1, 0).reshape(NB),
        ]).astype(jnp.int32)
        return tile_attention(meta, queries, halo)

    got_rows = shift(rows, "zh", 1)
    got = shift(give, "x", 2)
    pick_away = own_pick(panels, tap_pick, got, 1 - zh, p)
    att_send = attend(1 - zh)
    att_got = shift(att_send, "zh", 1)
    later_p = after(p, got, got_rows, att_send)
    width = panels.shape[1] // 2
    give = lax.dynamic_slice(panels, (zh * TILE, (1 - later_p) * width), (TILE, width))
    att_keep = attend(zh)
    own = after(alignment_own(rows, after(got_rows, att_send), x), att_keep, att_got)
    pick_here = own_pick(panels, tap_pick, after(shift(give, "x", 2), own), zh, p)
    arrived = shift(after(pick_away, att_got, own), "zh", 1)
    att = after(jnp.stack([att_keep, att_got]), own, pick_here)
    ahead, behind, far_low, far_high = ring_gather(att, "x")
    atts = (att, ahead, behind, far_low.reshape(TILE, TILE), far_high.reshape(TILE, TILE))
    parts = alignment_parts(own, y, arrived, far_low, far_high)
    tap = lax.dynamic_index_in_dim(tap_pick, zh, 0, keepdims=False)
    target = jnp.where(tap // 2 == zh, after(pick_here, ahead, behind), arrived)
    meta = jnp.stack([y, c, zl, x]).astype(jnp.int32)
    attn_terms, align_terms = gradients(meta, atts, parts, target)
    align_near = ring_near(align_terms, ring_far(align_terms, "y", attn_terms[0]), "y", "align_add_far")
    attn_near = ring_near(attn_terms, ring_far(attn_terms, "x", attn_terms[0]), "x", "attn_add_far")
    total = sum_terms(align_terms[0], *align_near).reshape(4, 2, 96, TILE)
    spread = sum_terms(total[0], *[shift(total[d], "zl", d) for d in (1, 2, 3)])
    attn_sum = sum_terms(attn_terms[0], *attn_near)
    attn_here = attn_sum[0]
    attn_away = shift(attn_sum[1], "zh", 1)
    grad_attn = jnp.concatenate([
        jnp.where(zh == 0, attn_here, attn_away),
        jnp.where(zh == 0, attn_away, attn_here),
    ])

    block = after(sum_terms(spread[0], shift(spread[1], "zh", 1)), attn_away)
    sizes = (2, 4, 4, 4, 2)
    moves = []
    for index in range(256):
        h, i, l, j, k = (int(n) for n in np.unravel_index(index, sizes))
        dest = (h, l, block_of(i), 2 * k + j // 2, j % 2)
        moves.append((index, int(np.ravel_multi_index(dest, sizes))))
    grad_align = lax.ppermute(block, SEG + SEQ, moves).T.astype(F32)
    return grad_align, grad_attn


def solution(mesh):
    fine = Mesh(mesh.devices.reshape(2, 4, 4, 4, 2), SEG + SEQ)
    placed = (
        P(SEQ, SEG),
        P(SEQ, SEG),
        P(SEQ, SEG),
        P(SEQ, None),
        P(SEQ),
        P(SEQ, SEG),
        P(SEG, None),
        P(SEQ),
    )
    return jax.shard_map(
        on_device,
        mesh=fine,
        in_specs=placed,
        out_specs=(P(SEG, SEQ), P(SEQ, SEG)),
        check_vma=False,
    )
```

```python
import jax
import jax.numpy as jnp
import numpy as np
from jax import lax
from jax.experimental import pallas as pl
from jax.experimental.pallas import tpu as pltpu
from jax.sharding import Mesh, PartitionSpec as P

HDIM = 128
TILE = 384
NB = 4
LOG2E = 1.4426950408889634
F32 = jnp.float32
BF16 = jnp.bfloat16
SEQ = ("zl", "y", "c")
SEG = ("zh", "x")
SMALL = pl.CostEstimate(flops=1, bytes_accessed=1, transcendentals=0)
PARAMS = pltpu.CompilerParams(vmem_limit_bytes=24 * 2**20)


def shift(a, axis, d):
    n = lax.axis_size(axis)
    return lax.ppermute(a, axis, [(i, (i + d) % n) for i in range(n)])


def after(value, *earlier):
    return lax.optimization_barrier((value, *earlier))[0]


def attn_kernel(meta, q_ref, before, here, after, out_ref, kvbuf, scores, sem):
    width = q_ref.shape[1]
    heads = width // HDIM
    count = meta[1]
    for half in range(2):
        cols = pl.ds(half * width, width)
        for j in range(NB):
            tile = meta[2 + j]
            for part, ref in enumerate((before, here, after)):
                @pl.when(tile // 2 == part)
                def _():
                    rows = pl.ds(pl.multiple_of((tile - 2 * part) * TILE, TILE), TILE)
                    pltpu.make_async_copy(ref.at[rows, cols], kvbuf.at[half, j], sem.at[half, j]).start()

    def arrive(half):
        for j in range(NB):
            cols = pl.ds(half * width, width)
            pltpu.make_async_copy(here.at[pl.ds(0, TILE), cols], kvbuf.at[half, j], sem.at[half, j]).wait()

    arrive(0)
    arrive(1)
    factor = HDIM ** (-0.5) * LOG2E
    for h in range(heads):
        cols = slice(h * HDIM, (h + 1) * HDIM)
        q = q_ref[:, cols]
        top = None
        for j in range(NB):
            s = lax.dot_general(q, kvbuf[0, j, :, cols], (((1,), (1,)), ((), ())), preferred_element_type=F32)
            if j >= 2:
                s = jnp.where(j < count, s, -jnp.inf)
            scores[:, j * TILE:(j + 1) * TILE] = s
            m = jnp.max(s, axis=1, keepdims=True)
            top = m if top is None else jnp.maximum(top, m)
        total = None
        acc = None
        for j in range(NB):
            e = jnp.exp2((scores[:, j * TILE:(j + 1) * TILE] - top) * factor)
            part = jnp.sum(e, axis=1, keepdims=True)
            total = part if total is None else total + part
            o = jnp.dot(e.astype(BF16), kvbuf[1, j, :, cols], preferred_element_type=F32)
            acc = o if acc is None else acc + o
        out_ref[:, cols] = (acc / total).astype(BF16)


def tile_attention(meta, queries, halo):
    width = queries.shape[1]
    grid_spec = pltpu.PrefetchScalarGridSpec(
        num_scalar_prefetch=1,
        grid=(1,),
        in_specs=[pl.BlockSpec((TILE, width), lambda i, meta: (meta[0], 0))]
        + [pl.BlockSpec(memory_space=pl.ANY)] * 3,
        out_specs=pl.BlockSpec((TILE, width), lambda i, meta: (0, 0)),
        scratch_shapes=[
            pltpu.VMEM((2, NB, TILE, width), BF16),
            pltpu.VMEM((TILE, NB * TILE), F32),
            pltpu.SemaphoreType.DMA((2, NB)),
        ],
    )
    return pl.pallas_call(
        attn_kernel,
        grid_spec=grid_spec,
        out_shape=jax.ShapeDtypeStruct((TILE, width), BF16),
        compiler_params=PARAMS,
        cost_estimate=SMALL,
        name="tile_attention",
    )(meta, queries, *halo)


def fetch_all(copies):
    for copy in copies:
        copy.start()
    return copies


def wait_all(copies):
    for copy in copies:
        copy.wait()


def part_copies(meta, parts, abuf, sem, cols, e):
    copies = []
    for n, ref in enumerate(parts):
        step = ref.shape[2]
        rows = pl.ds(pl.multiple_of(jnp.bitwise_xor(meta[1], n) * step, step), step)
        copies.append(pltpu.make_async_copy(ref.at[e, :, :, cols], abuf.at[e, :, rows, :], sem.at[e, n]))
    return copies


def slot_of(meta, j):
    return 2 * lax.rem(meta[3] + j % 4 + 4 - meta[2], 4) + j // 4


def transposed_product(meta, r, atts, write):
    r_t = r.T
    for j in range(8):
        val = jnp.dot(r_t, atts[j % 4, j // 4], preferred_element_type=F32)
        for k in range(4):
            write(lax.rem(k + 4 - meta[0], 4), slot_of(meta, j), val[96 * k:96 * (k + 1)])


def residual_kernel(meta, *refs):
    atts, parts = refs[:5], refs[5:7]
    target, res_ref, prod_ref, abuf, attbuf, sem, att_sem = refs[7:]
    slots = [attbuf.at[0], attbuf.at[1], attbuf.at[3], attbuf.at[2, 0], attbuf.at[2, 1]]
    off = pl.multiple_of(meta[4] * TILE, TILE)
    align_loads, att_loads = {}, {}
    for e, loads in ((0, (0,)), (1, (1,)), (3, (2,)), (2, (3, 4))):
        align_loads[e] = fetch_all(part_copies(meta, parts, abuf, sem, pl.ds(off, TILE), e))
        att_loads[e] = fetch_all([pltpu.make_async_copy(atts[n], slots[n], att_sem.at[n]) for n in loads])
    acc = -target[:, pl.ds(off, TILE)].astype(F32)
    for e in (0, 1, 3, 2):
        wait_all(align_loads[e])
        wait_all(att_loads[e])
        for z in range(2):
            acc = acc + jnp.dot(attbuf[e, z], abuf[e, z], preferred_element_type=F32)
    residual = acc.astype(BF16)
    res_ref[...] = residual

    def write(d, g, val):
        prod_ref[d, g] = val.astype(BF16)

    transposed_product(meta, residual, attbuf, write)


def attn_grad_kernel(meta, *refs):
    res_here, res_away, parts = refs[0], refs[1], refs[2:4]
    here, right, left, far_right, far_left = refs[5:10]
    abuf, sem = refs[10:]
    outs = [here.at[0], right.at[0], far_right, left.at[0], here.at[1], right.at[1], far_left, left.at[1]]
    order = (2, 1, 3, 0)
    loads = {e: fetch_all(part_copies(meta, parts, abuf, sem, pl.ds(0, 2 * TILE), e)) for e in order}
    first = meta[1] == 0
    low = jnp.where(first, res_here[...], res_away[...])
    high = jnp.where(first, res_away[...], res_here[...])
    contract = (((1,), (1,)), ((), ()))
    for e in order:
        wait_all(loads[e])
        for z in range(2):
            val = lax.dot_general(low, abuf[e, z, :, :TILE], contract, preferred_element_type=F32)
            val = val + lax.dot_general(high, abuf[e, z, :, TILE:], contract, preferred_element_type=F32)
            outs[4 * z + e][...] = val.astype(BF16)


def pair_kernel(own, arrived, here, right, left, far_right, far_left):
    def pair(d):
        return (own[d].astype(F32) + arrived[d].astype(F32)).astype(BF16)

    far = pair(2)
    far_right[...] = far[:4]
    far_left[...] = far[4:]
    right[...] = pair(1)
    left[...] = pair(3)
    here[...] = pair(0)


def add_far_kernel(right, left, from_left, from_right, right_out, left_out):
    half = right.shape[0] // 2
    right_out[half:] = right[half:]
    right_out[:half] = (right[:half].astype(F32) + from_left[...].astype(F32)).astype(BF16)
    left_out[:half] = left[:half]
    left_out[half:] = (left[half:].astype(F32) + from_right[...].astype(F32)).astype(BF16)


SMEM = pl.BlockSpec(memory_space=pltpu.SMEM)
VMEM = pl.BlockSpec(memory_space=pltpu.VMEM)
ANY = pl.BlockSpec(memory_space=pl.ANY)


def residual_half(meta, half, atts, parts, target, name):
    return pl.pallas_call(
        residual_kernel,
        in_specs=[SMEM] + [ANY] * 7 + [VMEM],
        out_specs=[VMEM] * 2,
        out_shape=[jax.ShapeDtypeStruct((TILE, TILE), BF16), jax.ShapeDtypeStruct((4, 8, 96, TILE), BF16)],
        scratch_shapes=[
            pltpu.VMEM((4, 2, TILE, TILE), BF16),
            pltpu.VMEM((4, 2, TILE, TILE), BF16),
            pltpu.SemaphoreType.DMA((4, 2)),
            pltpu.SemaphoreType.DMA((5,)),
        ],
        compiler_params=pltpu.CompilerParams(vmem_limit_bytes=60 * 2**20),
        cost_estimate=SMALL,
        name=name,
    )(jnp.concatenate([meta, half.reshape(1)]).astype(jnp.int32), *atts, *parts, target)


def gradients(meta, atts, parts, target):
    c = meta[1]
    away, product = residual_half(meta, 1 - c, atts, parts, target, "residual_away")
    arrived = shift(product, "c", 1)
    target = after(target, away)
    here, product = residual_half(meta, c, atts, parts, target, "residual_here")
    half_piece = jax.ShapeDtypeStruct((4, 96, TILE), BF16)
    whole_piece = jax.ShapeDtypeStruct((8, 96, TILE), BF16)
    keep, right, left, far_right, far_left = pl.pallas_call(
        pair_kernel,
        in_specs=[VMEM] * 2,
        out_specs=[VMEM] * 5,
        out_shape=[whole_piece] * 3 + [half_piece] * 2,
        compiler_params=PARAMS,
        cost_estimate=SMALL,
        name="core_pair_sum",
    )(product, arrived)
    partials = pl.pallas_call(
        attn_grad_kernel,
        in_specs=[SMEM, VMEM, VMEM] + [ANY] * 3,
        out_specs=[VMEM] * 5,
        out_shape=[jax.ShapeDtypeStruct((2, TILE, TILE), BF16)] * 3 + [jax.ShapeDtypeStruct((TILE, TILE), BF16)] * 2,
        scratch_shapes=[pltpu.VMEM((4, 2, TILE, 2 * TILE), BF16), pltpu.SemaphoreType.DMA((4, 2))],
        compiler_params=PARAMS,
        cost_estimate=SMALL,
        name="attn_grad_terms",
    )(meta, here, away, *parts, far_right)
    grad_terms = (keep, right, left, far_right, far_left)
    return partials, grad_terms


def ring_far(terms, axis, earlier):
    far_right, far_left = terms[3:]
    return after(shift(far_right, axis, 1), earlier), shift(far_left, axis, -1)


def ring_near(terms, arrived, axis, name):
    keep, right, left = terms[:3]
    arrived = [a.reshape((-1,) + right.shape[1:]) for a in arrived]
    right, left = pl.pallas_call(
        add_far_kernel,
        in_specs=[VMEM] * 4,
        out_specs=[VMEM] * 2,
        out_shape=[jax.ShapeDtypeStruct(right.shape, BF16)] * 2,
        compiler_params=PARAMS,
        cost_estimate=SMALL,
        name=name,
    )(right, left, *arrived)
    return shift(right, axis, 1), shift(left, axis, -1)


def sum_terms(*terms):
    total = terms[0].astype(F32)
    for term in terms[1:]:
        total = total + term.astype(F32)
    return total.astype(BF16)


def ring_gather(own, axis, *earlier):
    ahead, behind = shift(own, axis, -1), shift(own, axis, 1)
    half = own.shape[0] // 2
    far_low = shift(after(behind, *earlier)[:half], axis, 1)
    far_high = shift(after(ahead, *earlier)[half:], axis, -1)
    return ahead, behind, far_low, far_high


def block_of(x):
    return 2 * (x % 2) + x // 2


def copy_all_kernel(meta, plan, *refs):
    count = len(refs) - 1
    sem = refs[count]
    loads = [pltpu.make_async_copy(src, dst, sem.at[n]) for n, (src, dst) in enumerate(plan(meta, refs[:count]))]
    wait_all(fetch_all(loads))


def copy_all(meta, plan, copies, arrays, outs, name):
    return pl.pallas_call(
        lambda meta_ref, *refs: copy_all_kernel(meta_ref, plan, *refs),
        in_specs=[SMEM] + [ANY] * len(arrays),
        out_specs=[VMEM] * len(outs),
        out_shape=[jax.ShapeDtypeStruct(shape, BF16) for shape in outs],
        scratch_shapes=[pltpu.SemaphoreType.DMA((copies,))],
        compiler_params=pltpu.CompilerParams(vmem_limit_bytes=60 * 2**20),
        cost_estimate=SMALL,
        name=name,
    )(meta, *arrays)


def first_copies(meta, key_rows, value_rows, alignment, panels):
    tokens, width = key_rows.shape
    model = alignment.shape[1]
    block = panels.shape[1] // 2

    def plan(meta, refs):
        k, v, a, p, both, rows, give, later = refs
        cols = pl.ds(pl.multiple_of(meta[2] * block, block), block)
        return [
            (a.at[pl.ds(pl.multiple_of(meta[0] * 48, 48), 48)], rows),
            (k, both.at[:, pl.ds(0, width)]),
            (v, both.at[:, pl.ds(width, width)]),
            (p.at[pl.ds(pl.multiple_of(meta[1] * TILE, TILE), TILE), cols], give),
            (p.at[pl.ds(pl.multiple_of((1 - meta[1]) * TILE, TILE), TILE), cols], later),
        ]

    outs = [(tokens, 2 * width), (48, model), (TILE, block), (TILE, block)]
    return copy_all(meta, plan, 5, (key_rows, value_rows, alignment, panels), outs, "first_copies")


def alignment_own(rows, got_rows, x):
    width = rows.shape[1] // 4
    blocks = jnp.stack([block_of(lax.rem(x + 4 - e, 4)) for e in range(4)]).astype(jnp.int32)

    def plan(meta, refs):
        own, got = refs[:2]
        pairs = []
        for e in range(4):
            cols = pl.ds(pl.multiple_of(meta[e] * width, width), width)
            pairs += [(own.at[:, cols], refs[2 + e].at[0]), (got.at[:, cols], refs[2 + e].at[1])]
        return pairs

    pieces = copy_all(blocks, plan, 8, (rows, got_rows), [(2, 48, width)] * 4, "alignment_cut")
    return jnp.stack([shift(pieces[e], "x", -e) if e else pieces[0] for e in range(4)])


def alignment_parts(own, y, arrived, *earlier):
    width = own.shape[3]
    ahead, behind, far_low, far_high = ring_gather(own, "y")

    def assemble(meta, refs):
        def rows(d):
            return pl.ds(pl.multiple_of(lax.rem(meta[0] + d, 4) * 48, 48), 48)

        out = refs[5]
        return [
            (refs[0], out.at[:, :, rows(0), :]),
            (refs[1], out.at[:, :, rows(1), :]),
            (refs[2], out.at[:, :, rows(3), :]),
            (refs[3], out.at[pl.ds(0, 2), :, rows(2), :]),
            (refs[4], out.at[pl.ds(2, 2), :, rows(2), :]),
        ]

    arrays = (after(own, *earlier), ahead, behind, far_low, far_high)
    mine = copy_all(y.reshape(1), assemble, 5, arrays, [(4, 2, 192, width)], "alignment_rows")[0]
    return mine, shift(after(mine, arrived), "c", 1)


def own_pick(panels, tap_pick, got, tile, p):
    width = panels.shape[1] // 2
    rows = lax.dynamic_slice(panels, (tile * TILE, p * width), (TILE, width))
    tap = lax.dynamic_index_in_dim(tap_pick, tile, 0, keepdims=False)
    return jnp.where((tap & 1) == p, rows, got)


def on_device(queries, key_rows, value_rows, neighbours, tile_counts, panels, alignment, tap_pick):
    zh, x, zl, y, c = (lax.axis_index(name) for name in ("zh", "x", "zl", "y", "c"))
    seq = (zl * 4 + y) * 2 + c
    count = 32
    up = [(i, i + 1) for i in range(count - 1)]
    down = [(i + 1, i) for i in range(count - 1)]
    p = x // 2
    start = jnp.stack([4 * c + y, 1 - zh, 1 - p]).astype(jnp.int32)
    both, rows, give, later = first_copies(start, key_rows, value_rows, alignment, panels)
    halo = (lax.ppermute(both, SEQ, up), both, lax.ppermute(both, SEQ, down))
    local_ids = neighbours - (seq - 1) * 2

    def attend(tile):
        meta = jnp.concatenate([
            tile.reshape(1),
            lax.dynamic_slice_in_dim(tile_counts, tile, 1),
            lax.dynamic_slice_in_dim(local_ids, tile, 1, 0).reshape(NB),
        ]).astype(jnp.int32)
        return tile_attention(meta, queries, halo)

    got_rows = shift(rows, "zh", 1)
    got = shift(give, "x", 2)
    pick_away = own_pick(panels, tap_pick, got, 1 - zh, p)
    att_send = attend(1 - zh)
    att_got = shift(att_send, "zh", 1)
    later = after(later, got, got_rows, att_send)
    att_keep = attend(zh)
    own = after(alignment_own(rows, after(got_rows, att_send), x), att_keep, att_got)
    pick_here = own_pick(panels, tap_pick, after(shift(later, "x", 2), own), zh, p)
    arrived = shift(after(pick_away, att_got, own), "zh", 1)
    att = jnp.stack([att_keep, att_got])
    ahead, behind, far_low, far_high = ring_gather(att, "x", pick_here)
    atts = (att, ahead, behind, far_low.reshape(TILE, TILE), far_high.reshape(TILE, TILE))
    parts = alignment_parts(own, y, arrived, far_low, far_high)
    tap = lax.dynamic_index_in_dim(tap_pick, zh, 0, keepdims=False)
    target = jnp.where(tap // 2 == zh, after(pick_here, ahead, behind), arrived)
    meta = jnp.stack([y, c, zl, x]).astype(jnp.int32)
    attn_terms, align_terms = gradients(meta, atts, parts, target)
    align_near = ring_near(align_terms, ring_far(align_terms, "y", attn_terms[0]), "y", "align_add_far")
    attn_near = ring_near(attn_terms, ring_far(attn_terms, "x", attn_terms[0]), "x", "attn_add_far")
    total = sum_terms(align_terms[0], *align_near).reshape(4, 2, 96, TILE)
    spread = sum_terms(total[0], *[shift(total[d], "zl", d) for d in (1, 2, 3)])
    attn_sum = sum_terms(attn_terms[0], *attn_near)
    attn_here = attn_sum[0]
    attn_away = shift(attn_sum[1], "zh", 1)
    grad_attn = jnp.concatenate([
        jnp.where(zh == 0, attn_here, attn_away),
        jnp.where(zh == 0, attn_away, attn_here),
    ])

    block = sum_terms(spread[0], shift(spread[1], "zh", 1))
    sizes = (2, 4, 4, 4, 2)
    moves = []
    for index in range(256):
        h, i, l, j, k = (int(n) for n in np.unravel_index(index, sizes))
        dest = (h, l, block_of(i), 2 * k + j // 2, j % 2)
        moves.append((index, int(np.ravel_multi_index(dest, sizes))))
    grad_align = lax.ppermute(block, SEG + SEQ, moves).T.astype(F32)
    return grad_align, grad_attn


def solution(mesh):
    fine = Mesh(mesh.devices.reshape(2, 4, 4, 4, 2), SEG + SEQ)
    placed = (
        P(SEQ, SEG),
        P(SEQ, SEG),
        P(SEQ, SEG),
        P(SEQ, None),
        P(SEQ),
        P(SEQ, SEG),
        P(SEG, None),
        P(SEQ),
    )
    return jax.shard_map(
        on_device,
        mesh=fine,
        in_specs=placed,
        out_specs=(P(SEG, SEQ), P(SEQ, SEG)),
        check_vma=False,
    )
```

```python
import jax
import jax.numpy as jnp
import numpy as np
from jax import lax
from jax.experimental import pallas as pl
from jax.experimental.pallas import tpu as pltpu
from jax.sharding import Mesh, PartitionSpec as P

HDIM = 128
TILE = 384
NB = 4
LOG2E = 1.4426950408889634
F32 = jnp.float32
BF16 = jnp.bfloat16
SEQ = ("zl", "y", "c")
SEG = ("zh", "x")
SMALL = pl.CostEstimate(flops=1, bytes_accessed=1, transcendentals=0)
PARAMS = pltpu.CompilerParams(vmem_limit_bytes=24 * 2**20)


def shift(a, axis, d):
    n = lax.axis_size(axis)
    return lax.ppermute(a, axis, [(i, (i + d) % n) for i in range(n)])


def after(value, *earlier):
    return lax.optimization_barrier((value, *earlier))[0]


def attn_kernel(meta, q_ref, before, here, after, out_ref, kvbuf, scores, sem):
    width = q_ref.shape[1]
    heads = width // HDIM
    count = meta[1]
    for half in range(2):
        cols = pl.ds(half * width, width)
        for j in range(NB):
            tile = meta[2 + j]
            for part, ref in enumerate((before, here, after)):
                @pl.when(tile // 2 == part)
                def _():
                    rows = pl.ds(pl.multiple_of((tile - 2 * part) * TILE, TILE), TILE)
                    pltpu.make_async_copy(ref.at[rows, cols], kvbuf.at[half, j], sem.at[half, j]).start()

    def arrive(half):
        for j in range(NB):
            cols = pl.ds(half * width, width)
            pltpu.make_async_copy(here.at[pl.ds(0, TILE), cols], kvbuf.at[half, j], sem.at[half, j]).wait()

    arrive(0)
    arrive(1)
    factor = HDIM ** (-0.5) * LOG2E
    for h in range(heads):
        cols = slice(h * HDIM, (h + 1) * HDIM)
        q = q_ref[:, cols]
        top = None
        for j in range(NB):
            s = lax.dot_general(q, kvbuf[0, j, :, cols], (((1,), (1,)), ((), ())), preferred_element_type=F32)
            if j >= 2:
                s = jnp.where(j < count, s, -jnp.inf)
            scores[:, j * TILE:(j + 1) * TILE] = s
            m = jnp.max(s, axis=1, keepdims=True)
            top = m if top is None else jnp.maximum(top, m)
        total = None
        acc = None
        for j in range(NB):
            e = jnp.exp2((scores[:, j * TILE:(j + 1) * TILE] - top) * factor)
            part = jnp.sum(e, axis=1, keepdims=True)
            total = part if total is None else total + part
            o = jnp.dot(e.astype(BF16), kvbuf[1, j, :, cols], preferred_element_type=F32)
            acc = o if acc is None else acc + o
        out_ref[:, cols] = (acc / total).astype(BF16)


def tile_attention(meta, queries, halo):
    width = queries.shape[1]
    grid_spec = pltpu.PrefetchScalarGridSpec(
        num_scalar_prefetch=1,
        grid=(1,),
        in_specs=[pl.BlockSpec((TILE, width), lambda i, meta: (meta[0], 0))]
        + [pl.BlockSpec(memory_space=pl.ANY)] * 3,
        out_specs=pl.BlockSpec((TILE, width), lambda i, meta: (0, 0)),
        scratch_shapes=[
            pltpu.VMEM((2, NB, TILE, width), BF16),
            pltpu.VMEM((TILE, NB * TILE), F32),
            pltpu.SemaphoreType.DMA((2, NB)),
        ],
    )
    return pl.pallas_call(
        attn_kernel,
        grid_spec=grid_spec,
        out_shape=jax.ShapeDtypeStruct((TILE, width), BF16),
        compiler_params=PARAMS,
        cost_estimate=SMALL,
        name="tile_attention",
    )(meta, queries, *halo)


def fetch_all(copies):
    for copy in copies:
        copy.start()
    return copies


def wait_all(copies):
    for copy in copies:
        copy.wait()


def part_copies(meta, parts, abuf, sem, e):
    copies = []
    for n, ref in enumerate(parts):
        step = ref.shape[2]
        rows = pl.ds(pl.multiple_of(jnp.bitwise_xor(meta[1], n) * step, step), step)
        copies.append(pltpu.make_async_copy(ref.at[e], abuf.at[e, :, rows, :], sem.at[e, n]))
    return copies


def slot_of(meta, j):
    return 2 * lax.rem(meta[3] + j % 4 + 4 - meta[2], 4) + j // 4


def transposed_product(meta, r, atts, write):
    r_t = r.T
    for e in range(4):
        both = jnp.dot(r_t, atts[e], preferred_element_type=F32)
        for z in range(2):
            val = both[:, z * TILE:(z + 1) * TILE]
            for k in range(4):
                write(lax.rem(k + 4 - meta[0], 4), slot_of(meta, 4 * z + e), val[96 * k:96 * (k + 1)])


def residual_kernel(meta, *refs):
    here, ahead, behind, far_low, far_high = refs[:5]
    parts = refs[5:7]
    target, res_ref, prod_ref, abuf, attbuf, sem, att_sem = refs[7:]
    off = pl.multiple_of(meta[4] * TILE, TILE)
    sources = {
        0: (here.at[0], here.at[1]),
        1: (ahead.at[0], ahead.at[1]),
        3: (behind.at[0], behind.at[1]),
        2: (far_low, far_high),
    }
    loads = {}
    for e, pair in sources.items():
        loads[e] = part_copies(meta, parts, abuf, sem, e)
        for z in range(2):
            slot = attbuf.at[e, :, pl.ds(z * TILE, TILE)]
            loads[e].append(pltpu.make_async_copy(pair[z], slot, att_sem.at[e, z]))
        fetch_all(loads[e])
    acc = -target[:, pl.ds(off, TILE)].astype(F32)
    for e in sources:
        wait_all(loads[e])
        rows = abuf[e].reshape(2 * TILE, TILE)
        acc = acc + jnp.dot(attbuf[e], rows, preferred_element_type=F32)
    residual = acc.astype(BF16)
    res_ref[...] = residual

    def write(d, g, val):
        prod_ref[d, g] = val.astype(BF16)

    transposed_product(meta, residual, attbuf, write)


def attn_grad_kernel(meta, *refs):
    res_here, res_away, parts_here, parts_away = refs[0], refs[1], refs[2:4], refs[4:6]
    here, right, left, far_right, far_left = refs[7:12]
    abuf_here, abuf_away, sem_here, sem_away = refs[12:]
    outs = [here.at[0], right.at[0], far_right, left.at[0], here.at[1], right.at[1], far_left, left.at[1]]
    order = (2, 1, 3, 0)
    loads = {}
    for e in order:
        loads[e] = part_copies(meta, parts_here, abuf_here, sem_here, e)
        loads[e] += part_copies(meta, parts_away, abuf_away, sem_away, e)
        fetch_all(loads[e])
    contract = (((1,), (1,)), ((), ()))
    for e in order:
        wait_all(loads[e])
        for z in range(2):
            val = lax.dot_general(res_here[...], abuf_here[e, z], contract, preferred_element_type=F32)
            val = val + lax.dot_general(res_away[...], abuf_away[e, z], contract, preferred_element_type=F32)
            outs[4 * z + e][...] = val.astype(BF16)


def pair_kernel(own, arrived, here, right, left, far_right, far_left):
    def pair(d):
        return (own[d].astype(F32) + arrived[d].astype(F32)).astype(BF16)

    far = pair(2)
    far_right[...] = far[:4]
    far_left[...] = far[4:]
    right[...] = pair(1)
    left[...] = pair(3)
    here[...] = pair(0)


def add_far_kernel(right, left, from_left, from_right, right_out, left_out):
    half = right.shape[0] // 2
    right_out[half:] = right[half:]
    right_out[:half] = (right[:half].astype(F32) + from_left[...].astype(F32)).astype(BF16)
    left_out[:half] = left[:half]
    left_out[half:] = (left[half:].astype(F32) + from_right[...].astype(F32)).astype(BF16)


SMEM = pl.BlockSpec(memory_space=pltpu.SMEM)
VMEM = pl.BlockSpec(memory_space=pltpu.VMEM)
ANY = pl.BlockSpec(memory_space=pl.ANY)


def residual_half(meta, half, atts, parts, target, name):
    return pl.pallas_call(
        residual_kernel,
        in_specs=[SMEM] + [ANY] * 7 + [VMEM],
        out_specs=[VMEM] * 2,
        out_shape=[jax.ShapeDtypeStruct((TILE, TILE), BF16), jax.ShapeDtypeStruct((4, 8, 96, TILE), BF16)],
        scratch_shapes=[
            pltpu.VMEM((4, 2, TILE, TILE), BF16),
            pltpu.VMEM((4, TILE, 2 * TILE), BF16),
            pltpu.SemaphoreType.DMA((4, 2)),
            pltpu.SemaphoreType.DMA((4, 2)),
        ],
        compiler_params=pltpu.CompilerParams(vmem_limit_bytes=60 * 2**20),
        cost_estimate=SMALL,
        name=name,
    )(jnp.concatenate([meta, half.reshape(1)]).astype(jnp.int32), *atts, *parts, target)


def gradients(meta, atts, parts, target):
    c = meta[1]
    target = after(target, parts[1])
    away, product = residual_half(meta, 1 - c, atts, parts[2:], target, "residual_away")
    arrived = shift(product, "c", 1)
    target = after(target, away)
    here, product = residual_half(meta, c, atts, parts[:2], target, "residual_here")
    half_piece = jax.ShapeDtypeStruct((4, 96, TILE), BF16)
    whole_piece = jax.ShapeDtypeStruct((8, 96, TILE), BF16)
    keep, right, left, far_right, far_left = pl.pallas_call(
        pair_kernel,
        in_specs=[VMEM] * 2,
        out_specs=[VMEM] * 5,
        out_shape=[whole_piece] * 3 + [half_piece] * 2,
        compiler_params=PARAMS,
        cost_estimate=SMALL,
        name="core_pair_sum",
    )(product, arrived)
    partials = pl.pallas_call(
        attn_grad_kernel,
        in_specs=[SMEM, VMEM, VMEM] + [ANY] * 5,
        out_specs=[VMEM] * 5,
        out_shape=[jax.ShapeDtypeStruct((2, TILE, TILE), BF16)] * 3 + [jax.ShapeDtypeStruct((TILE, TILE), BF16)] * 2,
        scratch_shapes=[pltpu.VMEM((4, 2, TILE, TILE), BF16)] * 2 + [pltpu.SemaphoreType.DMA((4, 2))] * 2,
        compiler_params=PARAMS,
        cost_estimate=SMALL,
        name="attn_grad_terms",
    )(meta, here, away, *parts, far_right)
    grad_terms = (keep, right, left, far_right, far_left)
    return partials, grad_terms


def ring_far(terms, axis, earlier):
    far_right, far_left = terms[3:]
    return after(shift(far_right, axis, 1), earlier), shift(far_left, axis, -1)


def ring_near(terms, arrived, axis, name):
    keep, right, left = terms[:3]
    arrived = [a.reshape((-1,) + right.shape[1:]) for a in arrived]
    right, left = pl.pallas_call(
        add_far_kernel,
        in_specs=[VMEM] * 4,
        out_specs=[VMEM] * 2,
        out_shape=[jax.ShapeDtypeStruct(right.shape, BF16)] * 2,
        compiler_params=PARAMS,
        cost_estimate=SMALL,
        name=name,
    )(right, left, *arrived)
    return shift(right, axis, 1), shift(left, axis, -1)


def sum_terms(*terms):
    total = terms[0].astype(F32)
    for term in terms[1:]:
        total = total + term.astype(F32)
    return total.astype(BF16)


def ring_gather(own, axis, *earlier):
    ahead, behind = shift(own, axis, -1), shift(own, axis, 1)
    half = own.shape[0] // 2
    far_low = shift(after(behind, *earlier)[:half], axis, 1)
    far_high = shift(after(ahead, *earlier)[half:], axis, -1)
    return ahead, behind, far_low, far_high


def block_of(x):
    return 2 * (x % 2) + x // 2


def copy_all_kernel(meta, plan, *refs):
    count = len(refs) - 1
    sem = refs[count]
    loads = [pltpu.make_async_copy(src, dst, sem.at[n]) for n, (src, dst) in enumerate(plan(meta, refs[:count]))]
    wait_all(fetch_all(loads))


def copy_all(meta, plan, copies, arrays, outs, name):
    return pl.pallas_call(
        lambda meta_ref, *refs: copy_all_kernel(meta_ref, plan, *refs),
        in_specs=[SMEM] + [ANY] * len(arrays),
        out_specs=[VMEM] * len(outs),
        out_shape=[jax.ShapeDtypeStruct(shape, BF16) for shape in outs],
        scratch_shapes=[pltpu.SemaphoreType.DMA((copies,))],
        compiler_params=pltpu.CompilerParams(vmem_limit_bytes=60 * 2**20),
        cost_estimate=SMALL,
        name=name,
    )(meta, *arrays)


def first_copies(meta, key_rows, value_rows, alignment, panels):
    tokens, width = key_rows.shape
    model = alignment.shape[1]
    block = panels.shape[1] // 2

    def plan(meta, refs):
        k, v, a, p, both, rows, give, later = refs
        cols = pl.ds(pl.multiple_of(meta[2] * block, block), block)
        return [
            (a.at[pl.ds(pl.multiple_of(meta[0] * 48, 48), 48)], rows),
            (k, both.at[:, pl.ds(0, width)]),
            (v, both.at[:, pl.ds(width, width)]),
            (p.at[pl.ds(pl.multiple_of(meta[1] * TILE, TILE), TILE), cols], give),
            (p.at[pl.ds(pl.multiple_of((1 - meta[1]) * TILE, TILE), TILE), cols], later),
        ]

    outs = [(tokens, 2 * width), (48, model), (TILE, block), (TILE, block)]
    return copy_all(meta, plan, 5, (key_rows, value_rows, alignment, panels), outs, "first_copies")


def alignment_own(rows, got_rows, x):
    width = rows.shape[1] // 4
    blocks = jnp.stack([block_of(lax.rem(x + 4 - e, 4)) for e in range(4)]).astype(jnp.int32)

    def plan(meta, refs):
        own, got = refs[:2]
        pairs = []
        for e in range(4):
            cols = pl.ds(pl.multiple_of(meta[e] * width, width), width)
            pairs += [(own.at[:, cols], refs[2 + e].at[0]), (got.at[:, cols], refs[2 + e].at[1])]
        return pairs

    pieces = copy_all(blocks, plan, 8, (rows, got_rows), [(2, 48, width)] * 4, "alignment_cut")
    return jnp.stack([shift(pieces[e], "x", -e) if e else pieces[0] for e in range(4)])


def alignment_parts(own, y, c, arrived, *earlier):
    ahead, behind, far_low, far_high = ring_gather(own, "y")

    def assemble(meta, refs):
        def rows(d):
            return pl.ds(pl.multiple_of(lax.rem(meta[0] + d, 4) * 48, 48), 48)

        pairs = []
        for n in range(2):
            out = refs[5 + n]
            cols = pl.ds(pl.multiple_of(jnp.bitwise_xor(meta[1], n) * TILE, TILE), TILE)
            pairs += [
                (refs[0].at[:, :, :, cols], out.at[:, :, rows(0), :]),
                (refs[1].at[:, :, :, cols], out.at[:, :, rows(1), :]),
                (refs[2].at[:, :, :, cols], out.at[:, :, rows(3), :]),
                (refs[3].at[:, :, :, cols], out.at[pl.ds(0, 2), :, rows(2), :]),
                (refs[4].at[:, :, :, cols], out.at[pl.ds(2, 2), :, rows(2), :]),
            ]
        return pairs

    arrays = (after(own, *earlier), ahead, behind, far_low, far_high)
    shape = (4, 2, 192, TILE)
    here, away = copy_all(jnp.stack([y, c]).astype(jnp.int32), assemble, 10, arrays, [shape] * 2, "alignment_rows")
    got_away = shift(after(here, arrived), "c", 1)
    got_here = shift(after(away, arrived), "c", 1)
    return here, got_here, away, got_away


def own_pick(panels, tap_pick, got, tile, p):
    width = panels.shape[1] // 2
    rows = lax.dynamic_slice(panels, (tile * TILE, p * width), (TILE, width))
    tap = lax.dynamic_index_in_dim(tap_pick, tile, 0, keepdims=False)
    return jnp.where((tap & 1) == p, rows, got)


def on_device(queries, key_rows, value_rows, neighbours, tile_counts, panels, alignment, tap_pick):
    zh, x, zl, y, c = (lax.axis_index(name) for name in ("zh", "x", "zl", "y", "c"))
    seq = (zl * 4 + y) * 2 + c
    count = 32
    up = [(i, i + 1) for i in range(count - 1)]
    down = [(i + 1, i) for i in range(count - 1)]
    p = x // 2
    start = jnp.stack([4 * c + y, 1 - zh, 1 - p]).astype(jnp.int32)
    both, rows, give, later = first_copies(start, key_rows, value_rows, alignment, panels)
    halo = (lax.ppermute(both, SEQ, up), both, lax.ppermute(both, SEQ, down))
    local_ids = neighbours - (seq - 1) * 2

    def attend(tile):
        meta = jnp.concatenate([
            tile.reshape(1),
            lax.dynamic_slice_in_dim(tile_counts, tile, 1),
            lax.dynamic_slice_in_dim(local_ids, tile, 1, 0).reshape(NB),
        ]).astype(jnp.int32)
        return tile_attention(meta, queries, halo)

    got_rows = shift(rows, "zh", 1)
    got = shift(give, "x", 2)
    pick_away = own_pick(panels, tap_pick, got, 1 - zh, p)
    att_send = attend(1 - zh)
    att_got = shift(att_send, "zh", 1)
    later = after(later, got, got_rows, att_send)
    att_keep = attend(zh)
    own = after(alignment_own(rows, after(got_rows, att_send), x), att_keep, att_got)
    pick_here = own_pick(panels, tap_pick, after(shift(later, "x", 2), own), zh, p)
    arrived = shift(after(pick_away, att_got, own), "zh", 1)
    att = jnp.stack([att_keep, att_got])
    ahead, behind, far_low, far_high = ring_gather(att, "x", pick_here)
    atts = (att, ahead, behind, far_low.reshape(TILE, TILE), far_high.reshape(TILE, TILE))
    parts = alignment_parts(own, y, c, arrived, far_low, far_high)
    tap = lax.dynamic_index_in_dim(tap_pick, zh, 0, keepdims=False)
    target = jnp.where(tap // 2 == zh, after(pick_here, ahead, behind), arrived)
    meta = jnp.stack([y, c, zl, x]).astype(jnp.int32)
    attn_terms, align_terms = gradients(meta, atts, parts, target)
    align_near = ring_near(align_terms, ring_far(align_terms, "y", attn_terms[0]), "y", "align_add_far")
    attn_near = ring_near(attn_terms, ring_far(attn_terms, "x", attn_terms[0]), "x", "attn_add_far")
    total = sum_terms(align_terms[0], *align_near).reshape(4, 2, 96, TILE)
    spread = sum_terms(total[0], *[shift(total[d], "zl", d) for d in (1, 2, 3)])
    attn_sum = sum_terms(attn_terms[0], *attn_near)
    attn_here = attn_sum[0]
    attn_away = shift(attn_sum[1], "zh", 1)
    grad_attn = jnp.concatenate([
        jnp.where(zh == 0, attn_here, attn_away),
        jnp.where(zh == 0, attn_away, attn_here),
    ])

    block = sum_terms(spread[0], shift(spread[1], "zh", 1))
    sizes = (2, 4, 4, 4, 2)
    moves = []
    for index in range(256):
        h, i, l, j, k = (int(n) for n in np.unravel_index(index, sizes))
        dest = (h, l, block_of(i), 2 * k + j // 2, j % 2)
        moves.append((index, int(np.ravel_multi_index(dest, sizes))))
    grad_align = lax.ppermute(block, SEG + SEQ, moves).T.astype(F32)
    return grad_align, grad_attn


def solution(mesh):
    fine = Mesh(mesh.devices.reshape(2, 4, 4, 4, 2), SEG + SEQ)
    placed = (
        P(SEQ, SEG),
        P(SEQ, SEG),
        P(SEQ, SEG),
        P(SEQ, None),
        P(SEQ),
        P(SEQ, SEG),
        P(SEG, None),
        P(SEQ),
    )
    return jax.shard_map(
        on_device,
        mesh=fine,
        in_specs=placed,
        out_specs=(P(SEG, SEQ), P(SEQ, SEG)),
        check_vma=False,
    )
```

```python
import jax
import jax.numpy as jnp
import numpy as np
from jax import lax
from jax.experimental import pallas as pl
from jax.experimental.pallas import tpu as pltpu
from jax.sharding import Mesh, PartitionSpec as P

HDIM = 128
TILE = 384
NB = 4
LOG2E = 1.4426950408889634
F32 = jnp.float32
BF16 = jnp.bfloat16
SEQ = ("zl", "y", "c")
SEG = ("zh", "x")
SMALL = pl.CostEstimate(flops=1, bytes_accessed=1, transcendentals=0)
PARAMS = pltpu.CompilerParams(vmem_limit_bytes=24 * 2**20)


def shift(a, axis, d):
    n = lax.axis_size(axis)
    return lax.ppermute(a, axis, [(i, (i + d) % n) for i in range(n)])


def after(value, *earlier):
    return lax.optimization_barrier((value, *earlier))[0]


def attn_kernel(meta, q_ref, before, here, after, out_ref, kvbuf, scores, sem):
    width = q_ref.shape[1]
    heads = width // HDIM
    count = meta[1]
    for half in range(2):
        cols = pl.ds(half * width, width)
        for j in range(NB):
            tile = meta[2 + j]
            for part, ref in enumerate((before, here, after)):
                @pl.when(tile // 2 == part)
                def _():
                    rows = pl.ds(pl.multiple_of((tile - 2 * part) * TILE, TILE), TILE)
                    pltpu.make_async_copy(ref.at[rows, cols], kvbuf.at[half, j], sem.at[half, j]).start()

    def arrive(half):
        for j in range(NB):
            cols = pl.ds(half * width, width)
            pltpu.make_async_copy(here.at[pl.ds(0, TILE), cols], kvbuf.at[half, j], sem.at[half, j]).wait()

    arrive(0)
    arrive(1)
    factor = HDIM ** (-0.5) * LOG2E
    for h in range(heads):
        cols = slice(h * HDIM, (h + 1) * HDIM)
        q = q_ref[:, cols]
        top = None
        for j in range(NB):
            s = lax.dot_general(q, kvbuf[0, j, :, cols], (((1,), (1,)), ((), ())), preferred_element_type=F32)
            if j >= 2:
                s = jnp.where(j < count, s, -jnp.inf)
            scores[:, j * TILE:(j + 1) * TILE] = s
            m = jnp.max(s, axis=1, keepdims=True)
            top = m if top is None else jnp.maximum(top, m)
        total = None
        acc = None
        for j in range(NB):
            e = jnp.exp2((scores[:, j * TILE:(j + 1) * TILE] - top) * factor)
            part = jnp.sum(e, axis=1, keepdims=True)
            total = part if total is None else total + part
            o = jnp.dot(e.astype(BF16), kvbuf[1, j, :, cols], preferred_element_type=F32)
            acc = o if acc is None else acc + o
        out_ref[:, cols] = (acc / total).astype(BF16)


def tile_attention(meta, queries, halo):
    width = queries.shape[1]
    grid_spec = pltpu.PrefetchScalarGridSpec(
        num_scalar_prefetch=1,
        grid=(1,),
        in_specs=[pl.BlockSpec((TILE, width), lambda i, meta: (meta[0], 0))]
        + [pl.BlockSpec(memory_space=pl.ANY)] * 3,
        out_specs=pl.BlockSpec((TILE, width), lambda i, meta: (0, 0)),
        scratch_shapes=[
            pltpu.VMEM((2, NB, TILE, width), BF16),
            pltpu.VMEM((TILE, NB * TILE), F32),
            pltpu.SemaphoreType.DMA((2, NB)),
        ],
    )
    return pl.pallas_call(
        attn_kernel,
        grid_spec=grid_spec,
        out_shape=jax.ShapeDtypeStruct((TILE, width), BF16),
        compiler_params=PARAMS,
        cost_estimate=SMALL,
        name="tile_attention",
    )(meta, queries, *halo)


def fetch_all(copies):
    for copy in copies:
        copy.start()
    return copies


def wait_all(copies):
    for copy in copies:
        copy.wait()


def part_copies(meta, parts, abuf, sem, e):
    copies = []
    for n, ref in enumerate(parts):
        step = ref.shape[2]
        rows = pl.ds(pl.multiple_of(jnp.bitwise_xor(meta[1], n) * step, step), step)
        copies.append(pltpu.make_async_copy(ref.at[e], abuf.at[e, :, rows, :], sem.at[e, n]))
    return copies


def slot_of(meta, j):
    return 2 * lax.rem(meta[3] + j % 4 + 4 - meta[2], 4) + j // 4


def transposed_product(meta, r, atts, write):
    r_t = r.T
    for e in range(4):
        both = jnp.dot(r_t, atts[e], preferred_element_type=F32)
        for z in range(2):
            val = both[:, z * TILE:(z + 1) * TILE]
            for k in range(4):
                write(lax.rem(k + 4 - meta[0], 4), slot_of(meta, 4 * z + e), val[96 * k:96 * (k + 1)])


def residual_kernel(meta, *refs):
    here, ahead, behind, far_low, far_high = refs[:5]
    parts = refs[5:7]
    target, res_ref, prod_ref, abuf, attbuf, sem, att_sem = refs[7:]
    off = pl.multiple_of(meta[4] * TILE, TILE)
    sources = {
        0: (here.at[0], here.at[1]),
        1: (ahead.at[0], ahead.at[1]),
        3: (behind.at[0], behind.at[1]),
        2: (far_low, far_high),
    }
    loads = {}
    for e, pair in sources.items():
        loads[e] = part_copies(meta, parts, abuf, sem, e)
        for z in range(2):
            slot = attbuf.at[e, :, pl.ds(z * TILE, TILE)]
            loads[e].append(pltpu.make_async_copy(pair[z], slot, att_sem.at[e, z]))
        fetch_all(loads[e])
    acc = -target[:, pl.ds(off, TILE)].astype(F32)
    for e in sources:
        wait_all(loads[e])
        rows = abuf[e].reshape(2 * TILE, TILE)
        acc = acc + jnp.dot(attbuf[e], rows, preferred_element_type=F32)
    residual = acc.astype(BF16)
    res_ref[...] = residual

    def write(d, g, val):
        prod_ref[d, g] = val.astype(BF16)

    transposed_product(meta, residual, attbuf, write)


def attn_grad_kernel(meta, *refs):
    res_here, res_away, parts_here, parts_away = refs[0], refs[1], refs[2:4], refs[4:6]
    here, right, left, far_right, far_left = refs[7:12]
    abuf_here, abuf_away, sem_here, sem_away = refs[12:]
    outs = [here.at[0], right.at[0], far_right, left.at[0], here.at[1], right.at[1], far_left, left.at[1]]
    order = (2, 1, 3, 0)
    loads = {}
    for e in order:
        loads[e] = part_copies(meta, parts_here, abuf_here, sem_here, e)
        loads[e] += part_copies(meta, parts_away, abuf_away, sem_away, e)
        fetch_all(loads[e])
    contract = (((1,), (1,)), ((), ()))
    for e in order:
        wait_all(loads[e])
        for z in range(2):
            val = lax.dot_general(res_here[...], abuf_here[e, z], contract, preferred_element_type=F32)
            val = val + lax.dot_general(res_away[...], abuf_away[e, z], contract, preferred_element_type=F32)
            outs[4 * z + e][...] = val.astype(BF16)


def pair_kernel(own, arrived, here, right, left, far_right, far_left):
    def pair(d):
        return (own[d].astype(F32) + arrived[d].astype(F32)).astype(BF16)

    far = pair(2)
    far_right[...] = far[:4]
    far_left[...] = far[4:]
    right[...] = pair(1)
    left[...] = pair(3)
    here[...] = pair(0)


def add_far_kernel(right, left, from_left, from_right, right_out, left_out):
    half = right.shape[0] // 2
    right_out[half:] = right[half:]
    right_out[:half] = (right[:half].astype(F32) + from_left[...].astype(F32)).astype(BF16)
    left_out[:half] = left[:half]
    left_out[half:] = (left[half:].astype(F32) + from_right[...].astype(F32)).astype(BF16)


SMEM = pl.BlockSpec(memory_space=pltpu.SMEM)
VMEM = pl.BlockSpec(memory_space=pltpu.VMEM)
ANY = pl.BlockSpec(memory_space=pl.ANY)


def residual_half(meta, half, atts, parts, target, name):
    return pl.pallas_call(
        residual_kernel,
        in_specs=[SMEM] + [ANY] * 7 + [VMEM],
        out_specs=[VMEM] * 2,
        out_shape=[jax.ShapeDtypeStruct((TILE, TILE), BF16), jax.ShapeDtypeStruct((4, 8, 96, TILE), BF16)],
        scratch_shapes=[
            pltpu.VMEM((4, 2, TILE, TILE), BF16),
            pltpu.VMEM((4, TILE, 2 * TILE), BF16),
            pltpu.SemaphoreType.DMA((4, 2)),
            pltpu.SemaphoreType.DMA((4, 2)),
        ],
        compiler_params=pltpu.CompilerParams(vmem_limit_bytes=60 * 2**20),
        cost_estimate=SMALL,
        name=name,
    )(jnp.concatenate([meta, half.reshape(1)]).astype(jnp.int32), *atts, *parts, target)


def gradients(meta, atts, parts, target):
    c = meta[1]
    target = after(target, parts[1])
    away, product = residual_half(meta, 1 - c, atts, parts[2:], target, "residual_away")
    arrived = shift(product, "c", 1)
    target = after(target, away)
    here, product = residual_half(meta, c, atts, parts[:2], target, "residual_here")
    half_piece = jax.ShapeDtypeStruct((4, 96, TILE), BF16)
    whole_piece = jax.ShapeDtypeStruct((8, 96, TILE), BF16)
    keep, right, left, far_right, far_left = pl.pallas_call(
        pair_kernel,
        in_specs=[VMEM] * 2,
        out_specs=[VMEM] * 5,
        out_shape=[whole_piece] * 3 + [half_piece] * 2,
        compiler_params=PARAMS,
        cost_estimate=SMALL,
        name="core_pair_sum",
    )(product, arrived)
    partials = pl.pallas_call(
        attn_grad_kernel,
        in_specs=[SMEM, VMEM, VMEM] + [ANY] * 5,
        out_specs=[VMEM] * 5,
        out_shape=[jax.ShapeDtypeStruct((2, TILE, TILE), BF16)] * 3 + [jax.ShapeDtypeStruct((TILE, TILE), BF16)] * 2,
        scratch_shapes=[pltpu.VMEM((4, 2, TILE, TILE), BF16)] * 2 + [pltpu.SemaphoreType.DMA((4, 2))] * 2,
        compiler_params=PARAMS,
        cost_estimate=SMALL,
        name="attn_grad_terms",
    )(meta, here, away, *parts, far_right)
    grad_terms = (keep, right, left, far_right, far_left)
    return partials, grad_terms


def ring_far(terms, axis, earlier):
    far_right, far_left = terms[3:]
    return after(shift(far_right, axis, 1), earlier), shift(far_left, axis, -1)


def ring_near(terms, arrived, axis, name):
    keep, right, left = terms[:3]
    arrived = [a.reshape((-1,) + right.shape[1:]) for a in arrived]
    right, left = pl.pallas_call(
        add_far_kernel,
        in_specs=[VMEM] * 4,
        out_specs=[VMEM] * 2,
        out_shape=[jax.ShapeDtypeStruct(right.shape, BF16)] * 2,
        compiler_params=PARAMS,
        cost_estimate=SMALL,
        name=name,
    )(right, left, *arrived)
    return shift(right, axis, 1), shift(left, axis, -1)


def sum_terms(*terms):
    total = terms[0].astype(F32)
    for term in terms[1:]:
        total = total + term.astype(F32)
    return total.astype(BF16)


def ring_gather(own, axis, *earlier):
    ahead, behind = shift(own, axis, -1), shift(own, axis, 1)
    half = own.shape[0] // 2
    far_low = shift(after(behind, *earlier)[:half], axis, 1)
    far_high = shift(after(ahead, *earlier)[half:], axis, -1)
    return ahead, behind, far_low, far_high


def block_of(x):
    return 2 * (x % 2) + x // 2


def copy_all_kernel(meta, plan, *refs):
    count = len(refs) - 1
    sem = refs[count]
    loads = [pltpu.make_async_copy(src, dst, sem.at[n]) for n, (src, dst) in enumerate(plan(meta, refs[:count]))]
    wait_all(fetch_all(loads))


def copy_all(meta, plan, copies, arrays, outs, name):
    return pl.pallas_call(
        lambda meta_ref, *refs: copy_all_kernel(meta_ref, plan, *refs),
        in_specs=[SMEM] + [ANY] * len(arrays),
        out_specs=[VMEM] * len(outs),
        out_shape=[jax.ShapeDtypeStruct(shape, BF16) for shape in outs],
        scratch_shapes=[pltpu.SemaphoreType.DMA((copies,))],
        compiler_params=pltpu.CompilerParams(vmem_limit_bytes=(60 if name == "first_copies" else 24) * 2**20),
        cost_estimate=SMALL,
        name=name,
    )(meta, *arrays)


def first_copies(meta, key_rows, value_rows, alignment, panels):
    tokens, width = key_rows.shape
    model = alignment.shape[1]
    block = panels.shape[1] // 2

    def plan(meta, refs):
        k, v, a, p, both, rows, give, later = refs
        cols = pl.ds(pl.multiple_of(meta[2] * block, block), block)
        return [
            (a.at[pl.ds(pl.multiple_of(meta[0] * 48, 48), 48)], rows),
            (k, both.at[:, pl.ds(0, width)]),
            (v, both.at[:, pl.ds(width, width)]),
            (p.at[pl.ds(pl.multiple_of(meta[1] * TILE, TILE), TILE), cols], give),
            (p.at[pl.ds(pl.multiple_of((1 - meta[1]) * TILE, TILE), TILE), cols], later),
        ]

    outs = [(tokens, 2 * width), (48, model), (TILE, block), (TILE, block)]
    return copy_all(meta, plan, 5, (key_rows, value_rows, alignment, panels), outs, "first_copies")


def alignment_own(rows, got_rows, x):
    width = rows.shape[1] // 4
    blocks = jnp.stack([block_of(lax.rem(x + 4 - e, 4)) for e in range(4)]).astype(jnp.int32)

    def plan(meta, refs):
        own, got = refs[:2]
        pairs = []
        for e in range(4):
            cols = pl.ds(pl.multiple_of(meta[e] * width, width), width)
            pairs += [(own.at[:, cols], refs[2 + e].at[0]), (got.at[:, cols], refs[2 + e].at[1])]
        return pairs

    pieces = copy_all(blocks, plan, 8, (rows, got_rows), [(2, 48, width)] * 4, "alignment_cut")
    return jnp.stack([shift(pieces[e], "x", -e) if e else pieces[0] for e in range(4)])


def alignment_parts(own, y, c, arrived, *earlier):
    ahead, behind, far_low, far_high = ring_gather(own, "y")

    def assemble(meta, refs):
        def rows(d):
            return pl.ds(pl.multiple_of(lax.rem(meta[0] + d, 4) * 48, 48), 48)

        pairs = []
        for n in range(2):
            out = refs[5 + n]
            cols = pl.ds(pl.multiple_of(jnp.bitwise_xor(meta[1], n) * TILE, TILE), TILE)
            pairs += [
                (refs[0].at[:, :, :, cols], out.at[:, :, rows(0), :]),
                (refs[1].at[:, :, :, cols], out.at[:, :, rows(1), :]),
                (refs[2].at[:, :, :, cols], out.at[:, :, rows(3), :]),
                (refs[3].at[:, :, :, cols], out.at[pl.ds(0, 2), :, rows(2), :]),
                (refs[4].at[:, :, :, cols], out.at[pl.ds(2, 2), :, rows(2), :]),
            ]
        return pairs

    arrays = (after(own, *earlier), ahead, behind, far_low, far_high)
    shape = (4, 2, 192, TILE)
    here, away = copy_all(jnp.stack([y, c]).astype(jnp.int32), assemble, 10, arrays, [shape] * 2, "alignment_rows")
    got_away = shift(after(here, arrived), "c", 1)
    got_here = shift(after(away, arrived), "c", 1)
    return here, got_here, away, got_away


def own_pick(panels, tap_pick, got, tile, p):
    width = panels.shape[1] // 2
    rows = lax.dynamic_slice(panels, (tile * TILE, p * width), (TILE, width))
    tap = lax.dynamic_index_in_dim(tap_pick, tile, 0, keepdims=False)
    return jnp.where((tap & 1) == p, rows, got)


def on_device(queries, key_rows, value_rows, neighbours, tile_counts, panels, alignment, tap_pick):
    zh, x, zl, y, c = (lax.axis_index(name) for name in ("zh", "x", "zl", "y", "c"))
    seq = (zl * 4 + y) * 2 + c
    count = 32
    up = [(i, i + 1) for i in range(count - 1)]
    down = [(i + 1, i) for i in range(count - 1)]
    p = x // 2
    start = jnp.stack([4 * c + y, 1 - zh, 1 - p]).astype(jnp.int32)
    both, rows, give, later = first_copies(start, key_rows, value_rows, alignment, panels)
    halo = (lax.ppermute(both, SEQ, up), both, lax.ppermute(both, SEQ, down))
    local_ids = neighbours - (seq - 1) * 2

    def attend(tile):
        meta = jnp.concatenate([
            tile.reshape(1),
            lax.dynamic_slice_in_dim(tile_counts, tile, 1),
            lax.dynamic_slice_in_dim(local_ids, tile, 1, 0).reshape(NB),
        ]).astype(jnp.int32)
        return tile_attention(meta, queries, halo)

    got_rows = shift(rows, "zh", 1)
    got = shift(give, "x", 2)
    pick_away = own_pick(panels, tap_pick, got, 1 - zh, p)
    att_send = attend(1 - zh)
    att_got = shift(att_send, "zh", 1)
    later = after(later, got, got_rows, att_send)
    att_keep = attend(zh)
    own = after(alignment_own(rows, after(got_rows, att_send), x), att_keep, att_got)
    pick_here = own_pick(panels, tap_pick, after(shift(later, "x", 2), own), zh, p)
    arrived = shift(after(pick_away, att_got, own), "zh", 1)
    att = jnp.stack([att_keep, att_got])
    ahead, behind, far_low, far_high = ring_gather(att, "x", pick_here)
    atts = (att, ahead, behind, far_low.reshape(TILE, TILE), far_high.reshape(TILE, TILE))
    parts = alignment_parts(own, y, c, arrived, far_low, far_high)
    tap = lax.dynamic_index_in_dim(tap_pick, zh, 0, keepdims=False)
    target = jnp.where(tap // 2 == zh, after(pick_here, ahead, behind), arrived)
    meta = jnp.stack([y, c, zl, x]).astype(jnp.int32)
    attn_terms, align_terms = gradients(meta, atts, parts, target)
    align_near = ring_near(align_terms, ring_far(align_terms, "y", attn_terms[0]), "y", "align_add_far")
    attn_near = ring_near(attn_terms, ring_far(attn_terms, "x", attn_terms[0]), "x", "attn_add_far")
    total = sum_terms(align_terms[0], *align_near).reshape(4, 2, 96, TILE)
    spread = sum_terms(total[0], *[shift(total[d], "zl", d) for d in (1, 2, 3)])
    attn_sum = sum_terms(attn_terms[0], *attn_near)
    attn_here = attn_sum[0]
    attn_away = shift(attn_sum[1], "zh", 1)
    grad_attn = jnp.concatenate([
        jnp.where(zh == 0, attn_here, attn_away),
        jnp.where(zh == 0, attn_away, attn_here),
    ])

    block = sum_terms(spread[0], shift(spread[1], "zh", 1))
    sizes = (2, 4, 4, 4, 2)
    moves = []
    for index in range(256):
        h, i, l, j, k = (int(n) for n in np.unravel_index(index, sizes))
        dest = (h, l, block_of(i), 2 * k + j // 2, j % 2)
        moves.append((index, int(np.ravel_multi_index(dest, sizes))))
    grad_align = lax.ppermute(block, SEG + SEQ, moves).T.astype(F32)
    return grad_align, grad_attn


def solution(mesh):
    fine = Mesh(mesh.devices.reshape(2, 4, 4, 4, 2), SEG + SEQ)
    placed = (
        P(SEQ, SEG),
        P(SEQ, SEG),
        P(SEQ, SEG),
        P(SEQ, None),
        P(SEQ),
        P(SEQ, SEG),
        P(SEG, None),
        P(SEQ),
    )
    return jax.shard_map(
        on_device,
        mesh=fine,
        in_specs=placed,
        out_specs=(P(SEG, SEQ), P(SEQ, SEG)),
        check_vma=False,
    )
```
